32 devices in a mesh: tm: 8 (over y, x, core), batch: 4 (over z).
Axes of the slice: x: 2, y: 2, z: 4, core: 2. Of those that a mesh axis runs over, the one named last changes fastest.
Arguments:
- audio: bfloat16 [4, 24576, 512], P('batch', 'tm'), may hold values from -6 to 6
- conditioning: bfloat16 [4, 80, 24576], P('batch', None, 'tm'), may hold values from -6 to 6
- speaker_ids: int32 [4, 8], P('batch'), may hold values from 0 to 111
- seg_starts: int32 [4, 8], P('batch'), may hold values from 0 to 24575, as said below
- grad_residual: bfloat16 [4, 24576, 512], P('batch', 'tm'), may hold values from -6 to 6
- grad_skip: bfloat16 [4, 24576, 512], P('batch', 'tm'), may hold values from -6 to 6
- conv_weight: float32 [1024, 1024], P('batch', 'tm'), may hold values from -0.1875 to 0.1875
- conv_first: float32 [1024, 1024], P('batch', 'tm'), may hold values from -0.0014648438 to 0.0014648438
- conv_second: float32 [1024, 1024], P('batch', 'tm'), may hold values from 8.58894e-10 to 3.435576e-09
- cond_weight: float32 [80, 1024], P('batch', 'tm'), may hold values from -0.625 to 0.625
- cond_first: float32 [80, 1024], P('batch', 'tm'), may hold values from -0.0014648438 to 0.0014648438
- cond_second: float32 [80, 1024], P('batch', 'tm'), may hold values from 8.58894e-10 to 3.435576e-09
- speaker_table: float32 [112, 1024], P('batch', 'tm'), may hold values from -1.5 to 1.5
- table_first: float32 [112, 1024], P('batch', 'tm'), may hold values from -0.00015258789 to 0.00015258789
- table_second: float32 [112, 1024], P('batch', 'tm'), may hold values from 7.668696e-12 to 3.0674786e-11
- out_weight: float32 [512, 1024], P('batch', 'tm'), may hold values from -0.75 to 0.75
- out_first: float32 [512, 1024], P('batch', 'tm'), may hold values from -0.00036621094 to 0.00036621094
- out_second: float32 [512, 1024], P('batch', 'tm'), may hold values from 5.3680876e-11 to 2.147235e-10
Outputs:
- residual_out: bfloat16 [4, 24576, 512], P('batch', 'tm')
- skip_out: bfloat16 [4, 24576, 512], P('batch', 'tm')
- audio_grad: bfloat16 [4, 24576, 512], P('batch', 'tm')
- prenorm: float32 [], replicated
- conv_first_new: float32 [1024, 1024], P('batch', 'tm')
- conv_second_new: float32 [1024, 1024], P('batch', 'tm')
- conv_new: float32 [1024, 1024], P('batch', 'tm')
- cond_first_new: float32 [80, 1024], P('batch', 'tm')
- cond_second_new: float32 [80, 1024], P('batch', 'tm')
- cond_new: float32 [80, 1024], P('batch', 'tm')
- table_first_new: float32 [112, 1024], P('batch', 'tm')
- table_second_new: float32 [112, 1024], P('batch', 'tm')
- table_new: float32 [112, 1024], P('batch', 'tm')
- out_first_new: float32 [512, 1024], P('batch', 'tm')
- out_second_new: float32 [512, 1024], P('batch', 'tm')
- out_new: float32 [512, 1024], P('batch', 'tm')
The draws below stay inside these ranges and needn't reach their ends.
Inputs may be any that keep to these rules, and one draw needn't show every extreme that they name: `seg_starts`: each row's starts rise strictly from 0 at the first; the segment that begins at the second start holds samples of the first 3072 and of the last 3072 of its row.
All inputs are finite; a program needn't handle non-finite values.
Results may differ from the reference program's by a relative error of at most 0.0067.
Values may be sent and summed in bfloat16 or wider, within the bound.
A program may use at most 192 MiB of HBM per device.

```python
import math
import jax
import jax.numpy as jnp
import numpy as np
from jax import lax

RESIDUAL_WIDTH = 512
COND = 80
NSPK = 112
DILATION_SIZE = 256
NSEG = 8
STEP = 10
T_DEV = 3072
SAMPLES_PER_ROW = 24576
ROWS = 4


def draw_seg_starts(key, part):
    key = jax.random.fold_in(key, 11)
    keys = jax.random.split(key, 3)
    first_end = jax.random.randint(keys[0], (ROWS, 1), 1, T_DEV)
    long_end = SAMPLES_PER_ROW - T_DEV + jax.random.randint(keys[1], (ROWS, 1), 1, T_DEV // 2)
    stride = (SAMPLES_PER_ROW - long_end) // (NSEG - 2)
    ahead = jnp.arange(1, NSEG - 2, dtype=jnp.int32)[None, :]
    jitter = jax.random.randint(keys[2], (ROWS, NSEG - 3), 0, 1 << 20) % stride
    later = long_end + ahead * stride + jitter
    zeros_col = jnp.zeros((ROWS, 1), jnp.int32)
    return jnp.concatenate([zeros_col, first_end, long_end, later], axis=1).astype(jnp.int32)


def plant(drawn, stream_key, low, largest):
    longest = drawn.shape.index(max(drawn.shape))
    spots = []
    for shift in (0, 1):
        where = [jax.random.randint(jax.random.fold_in(stream_key, axis), (), 0, length) for axis, length in enumerate(drawn.shape)]
        where[longest] = (where[longest] + shift) % drawn.shape[longest]
        spots.append(tuple(where))
    return drawn.at[spots[0]].set(low).at[spots[1]].set(largest)


def block_scale(rng, extent, shards, smallest, top_value):
    loudness = 1.0
    for axis_at, parts in shards:
        draws = jax.random.uniform(jax.random.fold_in(jax.random.fold_in(rng, 6), axis_at), (parts,), jnp.float32, smallest / len(shards), top_value / len(shards))
        loudness = loudness * jnp.repeat(jnp.exp(draws), extent[axis_at] // parts).reshape((-1,) + (1,) * (len(extent) - 1 - axis_at))
    return loudness


def rank_table(amount, skew):
    weights = [(1 << 20) // math.isqrt(rank ** skew) + 1 for rank in range(1, amount + 1)]
    scale = 1 + sum(weights) // (1 << 30)
    return np.cumsum(np.array([max(1, weight // scale) for weight in weights]))


def skewed_ids(stream_key, extent, count, lean):
    grid = rank_table(count, lean)
    ticket = jax.random.randint(jax.random.fold_in(stream_key, 1), extent, 0, int(grid[count - 1]))
    rank = jnp.searchsorted(jnp.asarray(grid, jnp.int32), ticket, side="right")
    return jax.random.permutation(jax.random.fold_in(stream_key, 2), count)[rank].astype(jnp.int32)


def normal_values(rng, shape, deviation, bound, cuts=(), held_as=jnp.bfloat16):
    loudness = block_scale(rng, shape, cuts, -0.22, 0.18) if cuts else 1.0
    result = jax.random.normal(rng, shape, jnp.float32) * deviation * loudness
    return jnp.minimum(jnp.maximum(result, -bound), bound).astype(held_as)


def setup_inputs(seed: int = 0) -> dict:
    streams_of = jax.random.split(jax.random.key(seed), 19)
    audio = normal_values(streams_of[0], (ROWS, SAMPLES_PER_ROW, RESIDUAL_WIDTH), 1.0, 6.0, ((0, 4), (1, 8)))
    conditioning = normal_values(streams_of[1], (ROWS, COND, SAMPLES_PER_ROW), 1.0, 6.0, ((0, 4), (2, 8)))
    speaker_ids = plant(skewed_ids(streams_of[2], (ROWS, NSEG), NSPK, 2), jax.random.fold_in(streams_of[2], 3), 0, NSPK - 1).astype(jnp.int32)
    seg_starts = draw_seg_starts(jax.random.fold_in(streams_of[18], 71), 0)
    grad_residual = normal_values(streams_of[4], (ROWS, SAMPLES_PER_ROW, RESIDUAL_WIDTH), 1.0, 6.0, ((0, 4), (1, 8)))
    grad_skip = normal_values(streams_of[5], (ROWS, SAMPLES_PER_ROW, RESIDUAL_WIDTH), 1.0, 6.0, ((0, 4), (1, 8)))
    conv_weight = normal_values(streams_of[6], (2 * RESIDUAL_WIDTH, 2 * RESIDUAL_WIDTH), (2 * RESIDUAL_WIDTH) ** -0.5, 0.1875, ((0, 4), (1, 8)), jnp.float32)
    conv_first = normal_values(streams_of[7], (2 * RESIDUAL_WIDTH, 2 * RESIDUAL_WIDTH), (0.11 / (4 * RESIDUAL_WIDTH * RESIDUAL_WIDTH + 2 * RESIDUAL_WIDTH * COND + RESIDUAL_WIDTH * RESIDUAL_WIDTH // 8 + 2 * RESIDUAL_WIDTH) ** 0.5), 0.0014648438, ((0, 4), (1, 8)), jnp.float32)
    conv_second = jnp.clip(jnp.exp(math.log(3.435576045873745e-09) - 1.3862944 * jax.random.uniform(streams_of[8], (2 * RESIDUAL_WIDTH, 2 * RESIDUAL_WIDTH), jnp.float32) ** block_scale(streams_of[8], (2 * RESIDUAL_WIDTH, 2 * RESIDUAL_WIDTH), ((0, 4), (1, 8)), -0.2, 0.2)), 8.588940114684362e-10, 3.435576045873745e-09)
    cond_weight = normal_values(streams_of[9], (COND, 2 * RESIDUAL_WIDTH), COND ** -0.5, 0.625, ((0, 4), (1, 8)), jnp.float32)
    cond_first = normal_values(streams_of[10], (COND, 2 * RESIDUAL_WIDTH), (0.11 / (4 * RESIDUAL_WIDTH * RESIDUAL_WIDTH + 2 * RESIDUAL_WIDTH * COND + RESIDUAL_WIDTH * RESIDUAL_WIDTH // 8 + 2 * RESIDUAL_WIDTH) ** 0.5), 0.0014648438, ((0, 4), (1, 8)), jnp.float32)
    cond_second = jnp.clip(jnp.exp(math.log(3.435576045873745e-09) - 1.3862944 * jax.random.uniform(streams_of[11], (COND, 2 * RESIDUAL_WIDTH), jnp.float32) ** block_scale(streams_of[11], (COND, 2 * RESIDUAL_WIDTH), ((0, 4), (1, 8)), -0.2, 0.2)), 8.588940114684362e-10, 3.435576045873745e-09)
    speaker_table = normal_values(streams_of[12], (NSPK, 2 * RESIDUAL_WIDTH), 0.1, 1.5, ((0, 4), (1, 8)), jnp.float32)
    table_first = normal_values(streams_of[13], (NSPK, 2 * RESIDUAL_WIDTH), (0.11 / (NSPK * (4 * RESIDUAL_WIDTH * RESIDUAL_WIDTH + 2 * RESIDUAL_WIDTH * COND + RESIDUAL_WIDTH * RESIDUAL_WIDTH // 8 + 2 * RESIDUAL_WIDTH)) ** 0.5), 0.00015258789, ((0, 4), (1, 8)), jnp.float32)
    table_second = jnp.clip(jnp.exp(math.log(3.0674785628237444e-11) - 1.3862944 * jax.random.uniform(streams_of[14], (NSPK, 2 * RESIDUAL_WIDTH), jnp.float32) ** block_scale(streams_of[14], (NSPK, 2 * RESIDUAL_WIDTH), ((0, 4), (1, 8)), -0.2, 0.2)), 7.668696407059361e-12, 3.0674785628237444e-11)
    out_weight = normal_values(streams_of[15], (RESIDUAL_WIDTH, 2 * RESIDUAL_WIDTH), (RESIDUAL_WIDTH // 8) ** -0.5, 0.75, ((0, 4), (1, 8)), jnp.float32)
    out_first = normal_values(streams_of[16], (RESIDUAL_WIDTH, 2 * RESIDUAL_WIDTH), (0.028 / (4 * RESIDUAL_WIDTH * RESIDUAL_WIDTH + 2 * RESIDUAL_WIDTH * COND + RESIDUAL_WIDTH * RESIDUAL_WIDTH // 8 + 2 * RESIDUAL_WIDTH) ** 0.5), 0.00036621094, ((0, 4), (1, 8)), jnp.float32)
    out_second = jnp.clip(jnp.exp(math.log(2.1472350286710906e-10) - 1.3862944 * jax.random.uniform(streams_of[17], (RESIDUAL_WIDTH, 2 * RESIDUAL_WIDTH), jnp.float32) ** block_scale(streams_of[17], (RESIDUAL_WIDTH, 2 * RESIDUAL_WIDTH), ((0, 4), (1, 8)), -0.2, 0.2)), 5.3680875716777265e-11, 2.1472350286710906e-10)
    return {"audio": audio, "conditioning": conditioning, "speaker_ids": speaker_ids, "seg_starts": seg_starts, "grad_residual": grad_residual, "grad_skip": grad_skip, "conv_weight": conv_weight, "conv_first": conv_first, "conv_second": conv_second, "cond_weight": cond_weight, "cond_first": cond_first, "cond_second": cond_second, "speaker_table": speaker_table, "table_first": table_first, "table_second": table_second, "out_weight": out_weight, "out_first": out_first, "out_second": out_second}


@jax.custom_vjp
def low(v):
    return lax.optimization_barrier(v.astype(jnp.bfloat16)).astype(jnp.float32)

@jax.custom_vjp
def low_back(v):
    return v

def low_keep(v):
    return (low(v), None)

def low_pass(kept, grad):
    return (grad,)

def back_keep(v):
    return (v, None)

def back_low(kept, grad):
    return (low(grad),)
low.defvjp(low_keep, low_pass)
low_back.defvjp(back_keep, back_low)
clip_level = 1.0
beta_one = 0.9
beta_two = 0.999
adam_eps = 1e-08
decay_rate = 0.01
learn_rate = 0.1

def matmul(left, right):
    return jnp.dot(left, right, precision=lax.Precision.HIGHEST, preferred_element_type=jnp.float32)

def block_forward(weights, block_items):
    conv_low, cond_low, out_low, seg_embed = weights
    prev_b, audio_b, cond_b, hot_b = block_items
    channels = audio_b.shape[1]
    mixture = matmul(prev_b, conv_low[:channels]) + matmul(audio_b, conv_low[channels:])
    mixture = mixture + matmul(cond_b.T, cond_low) + matmul(hot_b, seg_embed)
    mixture = low_back(mixture)
    gated_out = low(jnp.tanh(mixture[:, :channels]) * jax.nn.sigmoid(mixture[:, channels:]))
    projected = matmul(gated_out, out_low)
    return (audio_b + projected[:, :channels], projected[:, channels:])

def adamw(gradient, factor, master, first_old, second_old):
    clipped = gradient * factor
    new_first = beta_one * first_old + (1.0 - beta_one) * clipped
    new_second = beta_two * second_old + (1.0 - beta_two) * clipped * clipped
    step_size = new_first / (1.0 - beta_one ** STEP) / (jnp.sqrt(new_second / (1.0 - beta_two ** STEP)) + adam_eps)
    new_master = master - learn_rate * (step_size + decay_rate * master)
    return (new_first, new_second, new_master)

def reference(audio, conditioning, speaker_ids, seg_starts, grad_residual, grad_skip, conv_weight, conv_first, conv_second, cond_weight, cond_first, cond_second, speaker_table, table_first, table_second, out_weight, out_first, out_second):
    positions = jnp.arange(SAMPLES_PER_ROW, dtype=jnp.int32)
    block_len = math.gcd(SAMPLES_PER_ROW, 4096)
    block_count = SAMPLES_PER_ROW // block_len
    masters = (conv_weight, cond_weight, speaker_table, out_weight)
    checked = jax.checkpoint(block_forward)

    def one_row(totals, row_items):
        audio_row, cond_row, ids_row, starts_row, dres_row, dskip_row = row_items
        segment = lax.optimization_barrier(jnp.sum((positions[:, None] >= starts_row[None, :]).astype(jnp.int32), axis=1)) - 1
        seg_match = segment[:, None] == jnp.arange(NSEG, dtype=jnp.int32)[None, :]
        local_start = lax.optimization_barrier(jnp.sum(jnp.where(seg_match, starts_row[None, :], 0), axis=1))
        retain_mask = (positions - DILATION_SIZE >= local_start).astype(jnp.float32)
        seg_hot = seg_match.astype(jnp.float32)
        speaker_hot = (ids_row[:, None] == jnp.arange(NSPK, dtype=jnp.int32)[None, :]).astype(jnp.float32)
        cond_float = cond_row.astype(jnp.float32)
        cond_blocks = cond_float.reshape(COND, block_count, block_len).transpose(1, 0, 2)
        hot_blocks = seg_hot.reshape(block_count, block_len, NSEG)

        def forward(audio_as_float, conv_master, cond_master, table_master, out_master):
            conv_low = low(conv_master)
            cond_low = low(cond_master)
            table_low = low(table_master)
            out_low = low(out_master)
            seg_embed = matmul(speaker_hot, table_low)
            delayed_input = jnp.concatenate([jnp.zeros((DILATION_SIZE, RESIDUAL_WIDTH), jnp.float32), audio_as_float[:SAMPLES_PER_ROW - DILATION_SIZE]], axis=0)
            previous = low_back(delayed_input * retain_mask[:, None])
            weights = (conv_low, cond_low, out_low, seg_embed)

            def run_block(block_items):
                return checked(weights, block_items)
            residual_blocks, skip_blocks = lax.map(run_block, (previous.reshape(block_count, block_len, RESIDUAL_WIDTH), audio_as_float.reshape(block_count, block_len, RESIDUAL_WIDTH), cond_blocks, hot_blocks))
            return (residual_blocks.reshape(SAMPLES_PER_ROW, RESIDUAL_WIDTH), skip_blocks.reshape(SAMPLES_PER_ROW, RESIDUAL_WIDTH))
        outputs, pullback = jax.vjp(forward, audio_row.astype(jnp.float32), conv_weight, cond_weight, speaker_table, out_weight)
        gradients = pullback((dres_row.astype(jnp.float32), dskip_row.astype(jnp.float32)))
        totals = tuple((total + gradient for total, gradient in zip(totals, gradients[1:])))
        return (totals, (outputs[0].astype(jnp.bfloat16), outputs[1].astype(jnp.bfloat16), gradients[0].astype(jnp.bfloat16)))
    start_sums = tuple((jnp.zeros(master.shape, jnp.float32) for master in masters))
    totals, (residual_out, skip_out, audio_grad) = lax.scan(one_row, start_sums, (audio, conditioning, speaker_ids, seg_starts, grad_residual, grad_skip))
    squares = jnp.sum(totals[0] * totals[0]) + jnp.sum(totals[1] * totals[1]) + jnp.sum(totals[2] * totals[2]) + jnp.sum(totals[3] * totals[3])
    prenorm = jnp.sqrt(squares)
    factor = jnp.minimum(1.0, clip_level / (prenorm + 1e-06))
    conv_state = adamw(totals[0], factor, conv_weight, conv_first, conv_second)
    cond_state = adamw(totals[1], factor, cond_weight, cond_first, cond_second)
    table_state = adamw(totals[2], factor, speaker_table, table_first, table_second)
    out_state = adamw(totals[3], factor, out_weight, out_first, out_second)
    return (residual_out, skip_out, audio_grad, prenorm, conv_state[0], conv_state[1], conv_state[2], cond_state[0], cond_state[1], cond_state[2], table_state[0], table_state[1], table_state[2], out_state[0], out_state[1], out_state[2])
```

```python
import functools

import jax
import jax.numpy as jnp
from jax import lax
from jax.experimental import pallas as pl
from jax.experimental.pallas import tpu as pltpu
from jax.sharding import PartitionSpec as P

DILATION_SIZE = 256
STEP = 10


clip_level = 1.0
beta_one = 0.9
beta_two = 0.999
adam_eps = 1e-08
decay_rate = 0.01
learn_rate = 0.1

LANES = 128
MESH = pl.DeviceIdType.MESH
BF16 = jnp.bfloat16
F32 = jnp.float32


def dot_nn(left, right):
    return lax.dot_general(left, right, (((1,), (0,)), ((), ())), preferred_element_type=F32)


def dot_nt(left, right):
    return lax.dot_general(left, right, (((1,), (1,)), ((), ())), preferred_element_type=F32)


def dot_tn(left, right):
    return lax.dot_general(left, right, (((0,), (0,)), ((), ())), preferred_element_type=F32)


def adamw(gradient, factor, master, first_old, second_old):
    clipped = gradient * factor
    new_first = beta_one * first_old + (1.0 - beta_one) * clipped
    new_second = beta_two * second_old + (1.0 - beta_two) * clipped * clipped
    step_size = (
        new_first
        / (1.0 - beta_one**STEP)
        / (jnp.sqrt(new_second / (1.0 - beta_two**STEP)) + adam_eps)
    )
    new_master = master - learn_rate * (step_size + decay_rate * master)
    return (new_first, new_second, new_master)


class Layer:
    def __init__(self, steps, channels, cond_dim, cond_rows, table_rows, seg_count):
        self.steps = steps
        self.channels = channels
        self.cond_dim = cond_dim
        self.cond_rows = cond_rows
        self.table_rows = table_rows
        self.seg_count = seg_count
        self.misc_rows = 64
        self.table_at = 32

    CHUNKS = ((0, 128), (512, 128), (1024, 64), (1280, 128))
    GRAD_ROWS = 1792

    def scratch(self):
        steps, ch = self.steps, self.channels
        wide = 2 * ch
        rows = self.GRAD_ROWS
        dma = pltpu.SemaphoreType.DMA
        return dict(
            ax=pltpu.VMEM((steps + DILATION_SIZE, ch), BF16),
            mp=pltpu.VMEM((steps, wide), F32),
            gg=pltpu.VMEM((steps, ch), F32),
            gated=pltpu.VMEM((steps, ch), BF16),
            mg=pltpu.VMEM((steps, wide), BF16),
            et=pltpu.VMEM((4 * self.misc_rows, steps), BF16),
            cn=pltpu.VMEM((self.cond_dim, steps), BF16),
            km=pltpu.VMEM((steps, LANES), F32),
            wb=pltpu.VMEM((4, 2, 128, wide), BF16),
            wo=pltpu.VMEM((4, 128, wide), BF16),
            wm=pltpu.VMEM((4, self.misc_rows, wide), BF16),
            conv_in=pltpu.VMEM((256, LANES), F32),
            out_in=pltpu.VMEM((128, LANES), F32),
            cond_in=pltpu.VMEM((self.cond_rows, LANES), F32),
            table_in=pltpu.VMEM((self.table_rows, LANES), F32),
            ss=pltpu.VMEM((rows, 4 * LANES), BF16),
            sr=pltpu.VMEM((rows, 4 * LANES), BF16),
            r1s=pltpu.VMEM((2, rows // 2, LANES), BF16),
            r1r=pltpu.VMEM((2, rows // 2, LANES), BF16),
            r3s=pltpu.VMEM((2, rows, LANES), BF16),
            r3r=pltpu.VMEM((2, rows, LANES), BF16),
            zs=pltpu.VMEM((rows, LANES), BF16),
            zr=pltpu.VMEM((3, rows // 4, LANES), BF16),
            phs=pltpu.VMEM((DILATION_SIZE, ch), BF16),
            phr=pltpu.VMEM((DILATION_SIZE, ch), BF16),
            nplane=pltpu.VMEM((8, 8, LANES), F32),
            nline=pltpu.VMEM((4, 8, LANES), F32),
            g_send=dma((4, 11)),
            g_recv=dma((4, 11)),
            r_send=dma((4, 8)),
            r_recv=dma((4, 8)),
            n_send=dma((10,)),
            n_recv=dma((10,)),
            h_send=dma((2,)),
            h_recv=dma((2,)),
            local=dma((8,)),
        )

    def kernel(
        self, ids, starts, audio, conditioning, grad_res, grad_skip, conv_w, cond_w, table_w, out_w, *rest
    ):
        names = list(self.scratch())
        outs, bufs = rest[: len(rest) - len(names)], rest[len(rest) - len(names) :]
        res, skip, agrad, fconv, fmisc, fout, norm = outs
        b = dict(zip(names, bufs))
        steps, ch = self.steps, self.channels
        ax, mp, gg, gated, mg = b["ax"], b["mp"], b["gg"], b["gated"], b["mg"]
        et, cn, km, wb, wo, wm = b["et"], b["cn"], b["km"], b["wb"], b["wo"], b["wm"]
        pv = res

        t = lax.axis_index("tm")
        z = lax.axis_index("batch")
        core = lax.rem(t, 2)
        chip = t // 2
        sib = t + 1 - 2 * core
        xbit = lax.rem(chip, 2)
        ybit = chip // 2
        xdelta = 1 - 2 * xbit
        ydelta = 2 * (1 - 2 * ybit)
        chip_x, chip_y, chip_d = chip + xdelta, chip + ydelta, chip + xdelta + ydelta
        tx, ty, td = 2 * chip_x + core, 2 * chip_y + core, 2 * chip_d + core
        zlow, zhigh = lax.rem(z, 2), z // 2
        zdelta = (1 - 2 * zlow, 2 * (1 - 2 * zhigh))
        zpeers = (z + zdelta[0], z + zdelta[1], z + zdelta[0] + zdelta[1])
        tlow, tmid, thigh = core, xbit, ybit

        def lanes(block):
            return pl.ds(pl.multiple_of(block * LANES, LANES), LANES)

        def rows_at(start, size):
            return pl.ds(pl.multiple_of(start, 16), size)

        def local(i, source, target):
            return pltpu.make_async_copy(source, target, b["local"].at[i])

        small = [
            local(0, conv_w, b["conv_in"]),
            local(1, out_w, b["out_in"]),
            local(2, cond_w, b["cond_in"]),
            local(3, table_w, b["table_in"]),
        ]
        own_ax = ax.at[pl.ds(DILATION_SIZE, steps), :]
        large = [
            local(4, audio.at[0], own_ax),
            local(5, conditioning.at[0], cn),
            local(6, grad_res.at[0], agrad),
            local(7, grad_skip.at[0], skip),
        ]
        for copy in small:
            copy.start()

        barrier = pltpu.get_barrier_semaphore()
        plane = []
        for k in range(1, 8):
            dt = (
                (1 - 2 * tlow) * (k & 1)
                + 2 * (1 - 2 * tmid) * ((k >> 1) & 1)
                + 4 * (1 - 2 * thigh) * ((k >> 2) & 1)
            )
            plane.append(t + dt)
        for peer in plane:
            pl.semaphore_signal(barrier, inc=1, device_id=(peer, z), device_id_type=MESH)
        for peer in zpeers:
            pl.semaphore_signal(barrier, inc=1, device_id=(t, peer), device_id_type=MESH)
        for copy in large:
            copy.start()

        for copy in small:
            copy.wait()
        for h in range(2):
            wb[z, h, :, lanes(t)] = b["conv_in"][h * 128 : (h + 1) * 128, :].astype(BF16)
        wo[z, :, lanes(t)] = b["out_in"][...].astype(BF16)
        pad_c = jnp.zeros((self.table_at - self.cond_rows, LANES), F32)
        pad_t = jnp.zeros((self.misc_rows - self.table_at - self.table_rows, LANES), F32)
        wm[z, :, lanes(t)] = jnp.concatenate(
            [b["cond_in"][...], pad_c, b["table_in"][...], pad_t], axis=0
        ).astype(BF16)
        pl.semaphore_wait(barrier, 10)

        def part(chunk, block, zs=None):
            whole = zs is None
            if chunk == 0:
                return wo.at[:, :, lanes(block)] if whole else wo.at[zs, :, lanes(block)]
            if chunk == 1:
                return wm.at[:, :, lanes(block)] if whole else wm.at[zs, :, lanes(block)]
            h = chunk - 2
            return wb.at[:, h, :, lanes(block)] if whole else wb.at[zs, h, :, lanes(block)]

        def push(ref, i, chunk, where):
            return pltpu.make_async_remote_copy(
                src_ref=ref,
                dst_ref=ref,
                send_sem=b["g_send"].at[chunk, i],
                recv_sem=b["g_recv"].at[chunk, i],
                device_id=where,
                device_id_type=MESH,
            )

        def g_copy(chunk, i):
            if i < 3:
                return push(part(chunk, t, pl.ds(z, 1)), i, chunk, (t, zpeers[i]))
            if i == 3:
                return push(part(chunk, t), i, chunk, (tx, z))
            if i == 4:
                return push(part(chunk, t), i, chunk, (ty, z))
            if i == 5:
                return push(part(chunk, tx, pl.ds(0, 2)), i, chunk, (ty, z))
            if i == 6:
                return push(part(chunk, ty, pl.ds(2, 2)), i, chunk, (tx, z))
            block = (t, tx, ty, td)[i - 7] if i < 11 else None
            return push(part(chunk, block), i, chunk, (sib, z))

        def g_start(chunk, i):
            g_copy(chunk, i).start()

        def g_wait(chunk, i):
            g_copy(chunk, i).wait_recv()

        def g_z(chunk):
            for i in range(3):
                g_start(chunk, i)

        def g_xy(chunk):
            for i in range(3):
                g_wait(chunk, i)
            for i in (3, 4, 7):
                g_start(chunk, i)

        def g_f(chunk):
            g_wait(chunk, 3)
            g_start(chunk, 5)
            g_start(chunk, 8)
            g_wait(chunk, 4)
            g_start(chunk, 6)
            g_start(chunk, 9)

        def g_d(chunk):
            g_wait(chunk, 5)
            g_wait(chunk, 6)
            g_start(chunk, 10)

        def g_s(chunk):
            for i in range(7, 11):
                g_wait(chunk, i)

        def halo_in():
            return pltpu.make_async_remote_copy(
                src_ref=audio.at[0, pl.ds(steps - DILATION_SIZE, DILATION_SIZE), :],
                dst_ref=ax.at[pl.ds(0, DILATION_SIZE), :],
                send_sem=b["h_send"].at[0],
                recv_sem=b["h_recv"].at[0],
                device_id=(jnp.minimum(t + 1, 7), z),
                device_id_type=MESH,
            )

        def halo_back():
            return pltpu.make_async_remote_copy(
                src_ref=b["phs"],
                dst_ref=b["phr"],
                send_sem=b["h_send"].at[1],
                recv_sem=b["h_recv"].at[1],
                device_id=(jnp.maximum(t - 1, 0), z),
                device_id_type=MESH,
            )

        def loop(count, body):
            lax.fori_loop(0, count, lambda i, c: (body(i), c)[1], 0)

        def make_mask():
            size = 256

            def body(i):
                at = rows_at(i * size, size)
                p = (
                    t * steps
                    + i * size
                    + lax.broadcasted_iota(jnp.int32, (size, LANES), 0)
                )
                drop = None
                for j in range(self.seg_count):
                    d = p - starts[0, j]
                    hit = (d >= 0) & (d < DILATION_SIZE)
                    drop = hit if drop is None else drop | hit
                km[at, :] = jnp.where(drop, 0.0, 1.0)

            loop(steps // size, body)

        def make_extra():
            cut = 1024
            n = self.misc_rows
            for c in range(steps // cut):
                at = pl.ds(c * cut, cut)
                p = t * steps + c * cut + lax.broadcasted_iota(jnp.int32, (1, cut), 1)
                speaker = jnp.full((1, cut), ids[0, 0], jnp.int32)
                for j in range(1, self.seg_count):
                    speaker = jnp.where(p >= starts[0, j], ids[0, j], speaker)
                wide_speaker = jnp.broadcast_to(speaker, (n, cut))
                for q in range(4):
                    row = lax.broadcasted_iota(jnp.int32, (n, self.cond_dim), 0)
                    col = lax.broadcasted_iota(jnp.int32, (n, self.cond_dim), 1)
                    pick = (col == row + q * self.cond_rows) & (row < self.cond_rows)
                    pick = jnp.where(pick, 1.0, 0.0).astype(BF16)
                    mel = dot_nn(pick, cn[:, at])
                    slot = lax.broadcasted_iota(jnp.int32, (n, cut), 0) - self.table_at
                    ours = (slot >= 0) & (slot < self.table_rows)
                    hot = ours & (slot + q * self.table_rows == wide_speaker)
                    et[q * n : (q + 1) * n, at] = jnp.where(hot, 1.0, mel).astype(BF16)

        def make_prev():
            size = 512

            def body(i):
                at = rows_at(i * size, size)
                keep = km[at, :].astype(BF16)
                pv[at, :] = ax[at, :] * jnp.concatenate([keep] * (ch // LANES), axis=1)

            loop(steps // size, body)

        def gated_grad():
            size = 1024

            def body(i):
                at = rows_at(i * size, size)
                w = wo[...].reshape(ch, 2 * ch)
                gg[at, :] = dot_nt(agrad[at, :], w[:, :ch]) + dot_nt(skip[at, :], w[:, ch:])

            loop(steps // size, body)

        def taps(i, size, h):
            at = rows_at(i * size, size)
            cur = pl.ds(pl.multiple_of(i * size + DILATION_SIZE, DILATION_SIZE), size)
            lo = slice(h * 128, h * 128 + 128)
            hi = slice(256 + h * 128, 256 + h * 128 + 128)
            return jnp.concatenate([pv[at, lo], pv[at, hi], ax[cur, lo], ax[cur, hi]], axis=1)

        def mixture_first():
            size = 1024

            def body(i):
                at = rows_at(i * size, size)
                lhs = taps(i, size, 0)
                cut = pl.ds(pl.multiple_of(i * size, size), size)
                for n in range(4):
                    cols = slice(n * 256, (n + 1) * 256)
                    w = wb[:, 0, :, cols].reshape(512, 256)
                    m = wm[:, :, cols].reshape(4 * self.misc_rows, 256)
                    mp[at, cols] = dot_nn(lhs, w) + dot_tn(et[:, cut], m)

            loop(steps // size, body)

        def gate():
            size = 1024

            def body(i):
                at = rows_at(i * size, size)
                lhs = taps(i, size, 1)
                for n in range(ch // 256):
                    c0 = slice(n * 256, (n + 1) * 256)
                    c1 = slice(ch + n * 256, ch + (n + 1) * 256)
                    x = mp[at, c0] + dot_nn(lhs, wb[:, 1, :, c0].reshape(512, 256))
                    y = mp[at, c1] + dot_nn(lhs, wb[:, 1, :, c1].reshape(512, 256))
                    th = jnp.tanh(x)
                    sg = 0.5 * jnp.tanh(0.5 * y) + 0.5
                    q = gg[at, c0]
                    g = th * sg
                    gated[at, c0] = g.astype(BF16)
                    mg[at, c0] = (q * (sg - g * th)).astype(BF16)
                    mg[at, c1] = (q * (g - g * sg)).astype(BF16)

            loop(steps // size, body)

        def wtaps(first):
            return wb[first : first + 2].reshape(ch, 2 * ch)

        def head_back():
            at = pl.ds(0, DILATION_SIZE)
            keep = jnp.concatenate([km[at, :]] * (ch // LANES), axis=1)
            b["phs"][...] = (keep * dot_nt(mg[at, :], wtaps(0))).astype(BF16)

            @pl.when(t > 0)
            def _():
                halo_back().start()

        def store_grad(row, value):
            size = value.shape[0]
            at = pl.ds(row, size)
            even = core == 0
            for k in range(4):
                left = value[:, 2 * k * LANES : (2 * k + 1) * LANES]
                right = value[:, (2 * k + 1) * LANES : (2 * k + 2) * LANES]
                cols = slice(k * LANES, (k + 1) * LANES)
                mp[at, cols] = jnp.where(even, left, right)
                b["ss"][at, cols] = jnp.where(even, right, left).astype(BF16)

        def conv_grad(h, side):
            lo = slice(h * 128, h * 128 + 128)
            hi = slice(256 + h * 128, 256 + h * 128 + 128)
            if side == 0:
                lhs = jnp.concatenate([pv[:, lo], pv[:, hi]], axis=1)
            else:
                cur = pl.ds(DILATION_SIZE, steps)
                lhs = jnp.concatenate([ax[cur, lo], ax[cur, hi]], axis=1)
            store_grad(512 * h + 256 * side, dot_tn(lhs, mg[...]))

        def misc_grad():
            store_grad(1024, dot_nn(et[...], mg[...]))

        def out_grad(side):
            lhs = gated[:, side * 256 : (side + 1) * 256]
            value = jnp.concatenate([dot_tn(lhs, agrad[...]), dot_tn(lhs, skip[...])], axis=1)
            store_grad(1280 + 256 * side, value)

        def projected(which):
            size = 1024

            def body(i):
                at = rows_at(i * size, size)
                if which == 0:
                    w = wo[:, :, :ch].reshape(ch, ch)
                    cur = pl.ds(pl.multiple_of(i * size + DILATION_SIZE, DILATION_SIZE), size)
                    res[at, :] = (ax[cur, :].astype(F32) + dot_nn(gated[at, :], w)).astype(BF16)
                else:
                    w = wo[:, :, ch:].reshape(ch, ch)
                    skip[at, :] = dot_nn(gated[at, :], w).astype(BF16)

            loop(steps // size, body)

        def audio_block(at, later):
            keep = jnp.concatenate([km[later, :]] * (ch // LANES), axis=1)
            total = agrad[at, :].astype(F32) + dot_nt(mg[at, :], wtaps(2))
            agrad[at, :] = (total + keep * dot_nt(mg[later, :], wtaps(0))).astype(BF16)

        def audio_main():
            def body(i):
                at = rows_at(i * 1024, 1024)
                later = pl.ds(pl.multiple_of(i * 1024 + DILATION_SIZE, DILATION_SIZE), 1024)
                audio_block(at, later)

            loop(2, body)

        def audio_rest():
            size = steps - 2048 - DILATION_SIZE
            audio_block(pl.ds(2048, size), pl.ds(2048 + DILATION_SIZE, size))

        def audio_last():
            @pl.when(t < 7)
            def _():
                halo_back().wait_recv()

            @pl.when(t == 7)
            def _():
                b["phr"][...] = jnp.zeros((DILATION_SIZE, ch), BF16)

            at = pl.ds(steps - DILATION_SIZE, DILATION_SIZE)
            total = agrad[at, :].astype(F32) + dot_nt(mg[at, :], wtaps(2))
            agrad[at, :] = (total + b["phr"][...].astype(F32)).astype(BF16)

        def r_copy(j, i):
            row, r = self.CHUNKS[j]
            if i == 0:
                at = pl.ds(row, 4 * r)
                source, target, where = b["ss"].at[at, :], b["sr"].at[at, :], (sib, z)
            elif i < 3:
                at = pl.ds(row // 2, 2 * r)
                source, target = b["r1s"].at[i - 1, at, :], b["r1r"].at[i - 1, at, :]
                where = (tx, z) if i == 1 else (ty, z)
            elif i < 5:
                at = pl.ds(row, 4 * r)
                source, target = b["r3s"].at[i - 3, at, :], b["r3r"].at[i - 3, at, :]
                where = (tx, z) if i == 3 else (ty, z)
            else:
                peer = zpeers[i - 5]
                source = b["zs"].at[rows_at(row + peer * r, r), :]
                target = b["zr"].at[i - 5, pl.ds(row // 4, r), :]
                where = (t, peer)
            return pltpu.make_async_remote_copy(
                src_ref=source,
                dst_ref=target,
                send_sem=b["r_send"].at[j, i],
                recv_sem=b["r_recv"].at[j, i],
                device_id=where,
                device_id_type=MESH,
            )

        def pair_sum(at, block):
            return mp[at, lanes(block)] + b["sr"][at, lanes(block)].astype(F32)

        def r_s(j):
            r_copy(j, 0).start()

        def r_1(j):
            row, r = self.CHUNKS[j]
            r_copy(j, 0).wait_recv()
            half = pl.ds(row // 2, 2 * r)
            b["r1s"][0, half, :] = pair_sum(pl.ds(row, 2 * r), chip_d).astype(BF16)
            r_copy(j, 1).start()
            b["r1s"][1, half, :] = pair_sum(pl.ds(row + 2 * r, 2 * r), chip_d).astype(BF16)
            r_copy(j, 2).start()

        def r_3(j):
            row, r = self.CHUNKS[j]
            up, low = pl.ds(row, 2 * r), pl.ds(row + 2 * r, 2 * r)
            half = pl.ds(row // 2, 2 * r)
            b["r3s"][0, up, :] = pair_sum(up, chip_x).astype(BF16)
            b["r3s"][1, low, :] = pair_sum(low, chip_y).astype(BF16)
            r_copy(j, 2).wait_recv()
            b["r3s"][0, low, :] = (
                pair_sum(low, chip_x) + b["r1r"][1, half, :].astype(F32)
            ).astype(BF16)
            r_copy(j, 3).start()
            r_copy(j, 1).wait_recv()
            b["r3s"][1, up, :] = (
                pair_sum(up, chip_y) + b["r1r"][0, half, :].astype(F32)
            ).astype(BF16)
            r_copy(j, 4).start()

        def plane_sum(at):
            return (
                pair_sum(at, chip)
                + b["r3r"][0, at, :].astype(F32)
                + b["r3r"][1, at, :].astype(F32)
            )

        def final(j):
            return (fconv.at[pl.ds(0, 128), :], fconv.at[pl.ds(128, 128), :], fmisc, fout)[j]

        def r_z(j):
            row, r = self.CHUNKS[j]
            r_copy(j, 3).wait_recv()
            r_copy(j, 4).wait_recv()
            at = pl.ds(row, 4 * r)
            b["zs"][at, :] = plane_sum(at).astype(BF16)
            for i in range(5, 8):
                r_copy(j, i).start()
            final(j)[...] = plane_sum(rows_at(row + z * r, r))

        def r_f(j):
            row, r = self.CHUNKS[j]
            total = final(j)[...]
            for i in range(5, 8):
                r_copy(j, i).wait_recv()
                total = total + b["zr"][i - 5, pl.ds(row // 4, r), :].astype(F32)
            final(j)[...] = total

        def tile_squares():
            total = jnp.zeros((8, LANES), F32)
            for j in range(4):
                value = final(j)[...]
                total = total + jnp.sum((value * value).reshape(-1, 8, LANES), axis=0)
            return total

        def n_copy(i):
            if i < 7:
                ref, where = b["nplane"].at[t], (plane[i], z)
            else:
                ref, where = b["nline"].at[z], (t, zpeers[i - 7])
            return pltpu.make_async_remote_copy(
                src_ref=ref,
                dst_ref=ref,
                send_sem=b["n_send"].at[i],
                recv_sem=b["n_recv"].at[i],
                device_id=where,
                device_id_type=MESH,
            )

        def norm_plane():
            b["nplane"][t] = tile_squares()
            for i in range(7):
                n_copy(i).start()

        def norm_line():
            for i in range(7):
                n_copy(i).wait_recv()
            total = b["nplane"][0]
            for k in range(1, 8):
                total = total + b["nplane"][k]
            b["nline"][z] = total
            for i in range(7, 10):
                n_copy(i).start()

        def norm_end():
            for i in range(7, 10):
                n_copy(i).wait_recv()
            total = b["nline"][0]
            for k in range(1, 4):
                total = total + b["nline"][k]
            norm[...] = total

        for chunk in (0, 1, 2, 3):
            g_z(chunk)

        @pl.when(t < 7)
        def _():
            halo_in().start()

        make_mask()
        large[1].wait()
        make_extra()
        large[0].wait()

        @pl.when(t == 0)
        def _():
            ax[pl.ds(0, DILATION_SIZE), :] = jnp.zeros((DILATION_SIZE, ch), BF16)

        g_xy(0)
        g_xy(1)
        g_xy(2)
        g_f(0)

        @pl.when(t > 0)
        def _():
            halo_in().wait_recv()

        make_prev()
        g_xy(3)
        g_f(1)
        g_d(0)
        g_f(2)
        large[2].wait()
        large[3].wait()
        g_s(0)
        gated_grad()
        g_f(3)
        g_d(1)
        g_d(2)
        g_s(1)
        g_s(2)
        mixture_first()
        g_d(3)
        g_s(3)
        gate()
        head_back()
        conv_grad(0, 0)
        conv_grad(0, 1)
        r_s(0)
        conv_grad(1, 0)
        r_1(0)
        conv_grad(1, 1)
        r_s(1)
        r_3(0)
        misc_grad()
        r_s(2)
        r_1(1)
        out_grad(0)
        r_z(0)
        r_3(1)
        r_1(2)
        out_grad(1)
        r_s(3)
        r_3(2)
        audio_main()
        r_1(3)
        r_z(1)
        r_z(2)
        r_f(0)
        audio_rest()
        r_3(3)
        audio_last()
        r_f(1)
        projected(0)
        r_z(3)
        r_f(2)
        projected(1)
        r_f(3)
        norm_plane()
        norm_line()
        norm_end()

        for chunk in range(4):
            for i in range(11):
                g_copy(chunk, i).wait_send()
        for j in range(4):
            for i in range(8):
                r_copy(j, i).wait_send()
        for i in range(10):
            n_copy(i).wait_send()

        @pl.when(t < 7)
        def _():
            halo_in().wait_send()

        @pl.when(t > 0)
        def _():
            halo_back().wait_send()

    def __call__(self, ids, starts, audio, conditioning, grad_res, grad_skip, conv_w, cond_w, table_w, out_w):
        steps, ch = self.steps, self.channels
        wide = pltpu.VMEM((steps, ch), BF16)
        smem = pl.BlockSpec(memory_space=pltpu.SMEM)
        anywhere = pl.BlockSpec(memory_space=pl.ANY)
        vmem = pl.BlockSpec(memory_space=pltpu.VMEM)
        return pl.pallas_call(
            self.kernel,
            out_shape=[
                wide,
                wide,
                wide,
                pltpu.VMEM((256, LANES), F32),
                pltpu.VMEM((self.misc_rows, LANES), F32),
                pltpu.VMEM((128, LANES), F32),
                pltpu.VMEM((8, LANES), F32),
            ],
            in_specs=[smem, smem] + [anywhere] * 8,
            out_specs=[vmem] * 7,
            scratch_shapes=list(self.scratch().values()),
            compiler_params=pltpu.CompilerParams(
                collective_id=0, has_side_effects=True, vmem_limit_bytes=52 * 2**20
            ),
            name="layer",
        )(ids, starts, audio, conditioning, grad_res, grad_skip, conv_w, cond_w, table_w, out_w)


def closing_kernel(cond_rows, table_at, table_rows, *refs):
    (res, skip, agrad, fconv, fmisc, fout, norm), refs = refs[:7], refs[7:]
    state, refs = refs[:12], refs[12:]
    (res_o, skip_o, agrad_o, prenorm_o), refs = refs[:4], refs[4:]
    new, (sems,) = refs[:12], refs[12:]
    copies = [
        pltpu.make_async_copy(source, target.at[0], sems.at[i])
        for i, (source, target) in enumerate(((res, res_o), (skip, skip_o), (agrad, agrad_o)))
    ]
    for copy in copies:
        copy.start()
    prenorm = jnp.sqrt(jnp.sum(norm[...], keepdims=True))
    prenorm_o[...] = prenorm
    factor = jnp.minimum(1.0, clip_level / (prenorm + 1e-06))
    grads = (
        fconv[...],
        fmisc[0:cond_rows, :],
        fmisc[table_at : table_at + table_rows, :],
        fout[...],
    )
    for k, grad in enumerate(grads):
        master, first, second = (state[3 * k + i][...] for i in range(3))
        for i, value in enumerate(adamw(grad, factor, master, first, second)):
            new[3 * k + i][...] = value
    for copy in copies:
        copy.wait()


def closing(layer, results, state):
    wide = jax.ShapeDtypeStruct((1, layer.steps, layer.channels), BF16)
    vmem = pl.BlockSpec(memory_space=pltpu.VMEM)
    anywhere = pl.BlockSpec(memory_space=pl.ANY)
    return pl.pallas_call(
        functools.partial(closing_kernel, layer.cond_rows, layer.table_at, layer.table_rows),
        out_shape=[wide, wide, wide, jax.ShapeDtypeStruct((1, 1), F32)]
        + [jax.ShapeDtypeStruct(a.shape, F32) for a in state],
        in_specs=[vmem] * 19,
        out_specs=[anywhere] * 3 + [vmem] * 13,
        scratch_shapes=[pltpu.SemaphoreType.DMA((3,))],
        compiler_params=pltpu.CompilerParams(vmem_limit_bytes=32 * 2**20),
        name="closing",
    )(*results, *state)


def on_device_kernels(
    audio,
    conditioning,
    speaker_ids,
    seg_starts,
    grad_residual,
    grad_skip,
    conv_weight,
    conv_first,
    conv_second,
    cond_weight,
    cond_first,
    cond_second,
    speaker_table,
    table_first,
    table_second,
    out_weight,
    out_first,
    out_second,
):
    layer = Layer(
        audio.shape[1],
        audio.shape[2],
        conditioning.shape[1],
        cond_weight.shape[0],
        speaker_table.shape[0],
        seg_starts.shape[1],
    )
    results = layer(
        speaker_ids,
        seg_starts,
        audio,
        conditioning,
        grad_residual,
        grad_skip,
        conv_weight,
        cond_weight,
        speaker_table,
        out_weight,
    )
    state = (
        conv_weight,
        conv_first,
        conv_second,
        cond_weight,
        cond_first,
        cond_second,
        speaker_table,
        table_first,
        table_second,
        out_weight,
        out_first,
        out_second,
    )
    done = closing(layer, results, state)
    return (done[0], done[1], done[2], done[3].reshape(()), *done[4:])


def passed_along(value, axis, steps):
    count = lax.axis_size(axis)
    first, last = (max(0, -steps), min(count, count - steps))
    return lax.ppermute(value, axis, [(source, source + steps) for source in range(first, last)])


def contract_rows(left, right):
    return lax.dot_general(
        left, right, (((0,), (0,)), ((), ())), preferred_element_type=jnp.float32
    )


def contract_cols(left, right):
    return lax.dot_general(
        left, right, (((1,), (1,)), ((), ())), preferred_element_type=jnp.float32
    )


def own_block(whole, shard):
    row_start = lax.axis_index("batch") * shard.shape[0]
    col_start = lax.axis_index("tm") * shard.shape[1]
    return lax.dynamic_slice(whole, (row_start, col_start), shard.shape)


def square_sum(matrix):
    return jnp.sum(matrix * matrix)


def on_device(
    audio,
    conditioning,
    speaker_ids,
    seg_starts,
    grad_residual,
    grad_skip,
    conv_weight,
    conv_first,
    conv_second,
    cond_weight,
    cond_first,
    cond_second,
    speaker_table,
    table_first,
    table_second,
    out_weight,
    out_first,
    out_second,
):
    rows_dev, steps_per_device, channels = audio.shape
    tokens = rows_dev * steps_per_device
    conv_rows, cond_rows, table_rows, out_rows = (
        lax.all_gather(conv_weight.astype(jnp.bfloat16), "batch", axis=0, tiled=True),
        lax.all_gather(cond_weight.astype(jnp.bfloat16), "batch", axis=0, tiled=True),
        lax.all_gather(speaker_table.astype(jnp.bfloat16), "batch", axis=0, tiled=True),
        lax.all_gather(out_weight.astype(jnp.bfloat16), "batch", axis=0, tiled=True),
    )
    conv_full, cond_full, table_full, out_full = (
        lax.all_gather(conv_rows, "tm", axis=1, tiled=True),
        lax.all_gather(cond_rows, "tm", axis=1, tiled=True),
        lax.all_gather(table_rows, "tm", axis=1, tiled=True),
        lax.all_gather(out_rows, "tm", axis=1, tiled=True),
    )
    offset = lax.axis_index("tm") * steps_per_device
    positions = offset + jnp.arange(steps_per_device, dtype=jnp.int32)
    seg_count = seg_starts.shape[1]
    segment = (
        jnp.sum((positions[None, :, None] >= seg_starts[:, None, :]).astype(jnp.int32), axis=2) - 1
    )
    seg_match = segment[:, :, None] == jnp.arange(seg_count, dtype=jnp.int32)[None, None, :]
    local_start = jnp.sum(jnp.where(seg_match, seg_starts[:, None, :], 0), axis=2)
    retain_mask = (positions[None, :] - DILATION_SIZE >= local_start).astype(jnp.bfloat16)
    seg_hot = seg_match.astype(jnp.bfloat16)
    speakers = table_full.shape[0]
    speaker_hot = (
        speaker_ids[:, :, None] == jnp.arange(speakers, dtype=jnp.int32)[None, None, :]
    ).astype(jnp.bfloat16)
    seg_embed = jnp.einsum(
        "rsk,kf->rsf", speaker_hot, table_full, preferred_element_type=jnp.float32
    ).astype(jnp.bfloat16)
    tail_input = passed_along(audio[:, steps_per_device - DILATION_SIZE :, :], "tm", 1)
    previous = (
        jnp.concatenate([tail_input, audio[:, : steps_per_device - DILATION_SIZE, :]], axis=1)
        * retain_mask[:, :, None]
    )
    flat_audio = audio.reshape(tokens, channels)
    flat_prev = previous.reshape(tokens, channels)
    mixture = jnp.dot(flat_prev, conv_full[:channels], preferred_element_type=jnp.float32)
    mixture = mixture + jnp.dot(
        flat_audio, conv_full[channels:], preferred_element_type=jnp.float32
    )
    mixture = mixture + jnp.einsum(
        "rct,cf->rtf", conditioning, cond_full, preferred_element_type=jnp.float32
    ).reshape(tokens, -1)
    mixture = mixture + jnp.einsum(
        "rts,rsf->rtf", seg_hot, seg_embed, preferred_element_type=jnp.float32
    ).reshape(tokens, -1)
    filter_tanh = jnp.tanh(mixture[:, :channels])
    gate_sig = jax.nn.sigmoid(mixture[:, channels:])
    gated_out = (filter_tanh * gate_sig).astype(jnp.bfloat16)
    projected = jnp.dot(gated_out, out_full, preferred_element_type=jnp.float32)
    residual_out = (
        (flat_audio.astype(jnp.float32) + projected[:, :channels])
        .astype(jnp.bfloat16)
        .reshape(audio.shape)
    )
    skip_out = projected[:, channels:].astype(jnp.bfloat16).reshape(audio.shape)
    back_out = jnp.concatenate(
        [grad_residual.reshape(tokens, channels), grad_skip.reshape(tokens, channels)], axis=1
    )
    out_grad = contract_rows(gated_out, back_out)
    gated_grad = contract_cols(back_out, out_full)
    filter_grad = gated_grad * gate_sig * (1.0 - filter_tanh * filter_tanh)
    gate_grad = gated_grad * filter_tanh * gate_sig * (1.0 - gate_sig)
    mixture_grad = jnp.concatenate([filter_grad, gate_grad], axis=1).astype(jnp.bfloat16)
    conv_grad = jnp.concatenate(
        [contract_rows(flat_prev, mixture_grad), contract_rows(flat_audio, mixture_grad)], axis=0
    )
    grad_blocks = mixture_grad.reshape(rows_dev, steps_per_device, -1)
    cond_grad = jnp.einsum(
        "rct,rtf->cf", conditioning, grad_blocks, preferred_element_type=jnp.float32
    )
    seg_sums = jnp.einsum("rts,rtf->rsf", seg_hot, grad_blocks, preferred_element_type=jnp.float32)
    table_grad = jnp.einsum(
        "rsk,rsf->kf",
        speaker_hot.astype(jnp.float32),
        seg_sums,
        precision=lax.Precision.HIGHEST,
        preferred_element_type=jnp.float32,
    )
    preceding_gradient = (
        contract_cols(mixture_grad, conv_full[:channels]).reshape(audio.shape)
        * retain_mask[:, :, None]
    ).astype(jnp.bfloat16)
    head_input = passed_along(preceding_gradient[:, :DILATION_SIZE, :], "tm", -1)
    later_contribution = jnp.concatenate(
        [preceding_gradient[:, DILATION_SIZE:, :], head_input], axis=1
    ).astype(jnp.float32)
    current_tap = contract_cols(mixture_grad, conv_full[channels:]).reshape(audio.shape)
    audio_grad = (grad_residual.astype(jnp.float32) + current_tap + later_contribution).astype(
        jnp.bfloat16
    )
    conv_total, cond_total, table_total, out_total = lax.psum(
        (conv_grad, cond_grad, table_grad, out_grad), ("tm", "batch")
    )
    squares = (
        square_sum(conv_total)
        + square_sum(cond_total)
        + square_sum(table_total)
        + square_sum(out_total)
    )
    conv_part = own_block(conv_total, conv_weight)
    cond_part = own_block(cond_total, cond_weight)
    table_part = own_block(table_total, speaker_table)
    out_part = own_block(out_total, out_weight)
    prenorm = jnp.sqrt(squares)
    factor = jnp.minimum(1.0, clip_level / (prenorm + 1e-06))
    conv_state = adamw(conv_part, factor, conv_weight, conv_first, conv_second)
    cond_state = adamw(cond_part, factor, cond_weight, cond_first, cond_second)
    table_state = adamw(table_part, factor, speaker_table, table_first, table_second)
    out_state = adamw(out_part, factor, out_weight, out_first, out_second)
    return (
        residual_out,
        skip_out,
        audio_grad,
        prenorm,
        conv_state[0],
        conv_state[1],
        conv_state[2],
        cond_state[0],
        cond_state[1],
        cond_state[2],
        table_state[0],
        table_state[1],
        table_state[2],
        out_state[0],
        out_state[1],
        out_state[2],
    )


def solution(mesh):
    placed = (
        P("batch", "tm", None),
        P("batch", None, "tm"),
        P("batch", None),
        P("batch", None),
        P("batch", "tm", None),
        P("batch", "tm", None),
        P("batch", "tm"),
        P("batch", "tm"),
        P("batch", "tm"),
        P("batch", "tm"),
        P("batch", "tm"),
        P("batch", "tm"),
        P("batch", "tm"),
        P("batch", "tm"),
        P("batch", "tm"),
        P("batch", "tm"),
        P("batch", "tm"),
        P("batch", "tm"),
    )
    small = mesh.shape["tm"] == 8 and mesh.shape["batch"] == 4
    return jax.shard_map(
        on_device_kernels if small else on_device,
        mesh=mesh,
        in_specs=placed,
        out_specs=(
            P("batch", "tm", None),
            P("batch", "tm", None),
            P("batch", "tm", None),
            P(),
            P("batch", "tm"),
            P("batch", "tm"),
            P("batch", "tm"),
            P("batch", "tm"),
            P("batch", "tm"),
            P("batch", "tm"),
            P("batch", "tm"),
            P("batch", "tm"),
            P("batch", "tm"),
            P("batch", "tm"),
            P("batch", "tm"),
            P("batch", "tm"),
        ),
        check_vma=False,
    )
```

```python
import functools

import jax
import jax.numpy as jnp
from jax import lax
from jax.experimental import pallas as pl
from jax.experimental.pallas import tpu as pltpu
from jax.sharding import PartitionSpec as P

DILATION_SIZE = 256
STEP = 10


clip_level = 1.0
beta_one = 0.9
beta_two = 0.999
adam_eps = 1e-08
decay_rate = 0.01
learn_rate = 0.1

LANES = 128
MESH = pl.DeviceIdType.MESH
BF16 = jnp.bfloat16
F32 = jnp.float32


def dot_nn(left, right):
    return lax.dot_general(left, right, (((1,), (0,)), ((), ())), preferred_element_type=F32)


def dot_nt(left, right):
    return lax.dot_general(left, right, (((1,), (1,)), ((), ())), preferred_element_type=F32)


def dot_tn(left, right):
    return lax.dot_general(left, right, (((0,), (0,)), ((), ())), preferred_element_type=F32)


def adamw(gradient, factor, master, first_old, second_old):
    clipped = gradient * factor
    new_first = beta_one * first_old + (1.0 - beta_one) * clipped
    new_second = beta_two * second_old + (1.0 - beta_two) * clipped * clipped
    step_size = (
        new_first
        / (1.0 - beta_one**STEP)
        / (jnp.sqrt(new_second / (1.0 - beta_two**STEP)) + adam_eps)
    )
    new_master = master - learn_rate * (step_size + decay_rate * master)
    return (new_first, new_second, new_master)


class Layer:
    def __init__(self, steps, channels, cond_dim, cond_rows, table_rows, seg_count):
        self.steps = steps
        self.channels = channels
        self.cond_dim = cond_dim
        self.cond_rows = cond_rows
        self.table_rows = table_rows
        self.seg_count = seg_count
        self.misc_rows = 64
        self.table_at = 32

    BLOCK_ROWS = 320
    PARTS = ((0, 160), (160, 160))
    CHUNK = 256
    PAIRS = (0, 1, 0, 1, 0, 1, None)
    GRAD_ROWS = 7 * 256

    def scratch(self):
        steps, ch = self.steps, self.channels
        wide = 2 * ch
        rows = self.GRAD_ROWS
        dma = pltpu.SemaphoreType.DMA
        return dict(
            taps=pltpu.VMEM((2, steps, ch), BF16),
            halo=pltpu.VMEM((DILATION_SIZE, ch), BF16),
            act=pltpu.VMEM((steps, wide), F32),
            own=pltpu.VMEM((2 * self.CHUNK, 4 * LANES), F32),
            gated=pltpu.VMEM((steps, ch), BF16),
            mg=pltpu.VMEM((steps, wide), BF16),
            et=pltpu.VMEM((4 * self.misc_rows, steps), BF16),
            extra=pltpu.VMEM((steps, 4 * self.misc_rows), BF16),
            cn=pltpu.VMEM((self.cond_dim, steps), BF16),
            km=pltpu.VMEM((steps, LANES), BF16),
            wall=pltpu.VMEM((4, self.BLOCK_ROWS, wide), BF16),
            wo=pltpu.VMEM((4, 128, wide), BF16),
            cond_in=pltpu.VMEM((self.cond_rows, LANES), F32),
            table_in=pltpu.VMEM((self.table_rows, LANES), F32),
            ss=pltpu.VMEM((rows, 4 * LANES), BF16),
            sr=pltpu.VMEM((rows, 4 * LANES), BF16),
            r1s=pltpu.VMEM((2, rows // 2, LANES), BF16),
            r1r=pltpu.VMEM((2, rows // 2, LANES), BF16),
            r3s=pltpu.VMEM((2, rows, LANES), BF16),
            r3r=pltpu.VMEM((2, rows, LANES), BF16),
            zs=pltpu.VMEM((rows, LANES), BF16),
            zr=pltpu.VMEM((3, 4 * 128, LANES), BF16),
            phs=pltpu.VMEM((DILATION_SIZE, ch), BF16),
            phr=pltpu.VMEM((DILATION_SIZE, ch), BF16),
            squares=pltpu.VMEM((32, 1, LANES), F32),
            g_recv=dma((43,)),
            r_recv=dma((7, 4)),
            h_recv=dma((2,)),
            sent=dma((7,)),
            n_recv=dma,
            local=dma((8,)),
        )

    def kernel(
        self, ids, starts, audio, conditioning, grad_res, grad_skip, conv_w, cond_w, table_w, out_w, *rest
    ):
        names = list(self.scratch())
        outs, bufs = rest[: len(rest) - len(names)], rest[len(rest) - len(names) :]
        res, skip, agrad, fconv, fmisc, fout, norm = outs
        b = dict(zip(names, bufs))
        steps, ch = self.steps, self.channels
        taps, act, own, gated, mg = b["taps"], b["act"], b["own"], b["gated"], b["mg"]
        et, extra, cn, km, wall, wo = b["et"], b["extra"], b["cn"], b["km"], b["wall"], b["wo"]

        t = lax.axis_index("tm")
        z = lax.axis_index("batch")
        core = lax.rem(t, 2)
        chip = t // 2
        sib = t + 1 - 2 * core
        xbit = lax.rem(chip, 2)
        ybit = chip // 2
        xdelta = 1 - 2 * xbit
        ydelta = 2 * (1 - 2 * ybit)
        chip_x, chip_y, chip_d = chip + xdelta, chip + ydelta, chip + xdelta + ydelta
        tx, ty, td = 2 * chip_x + core, 2 * chip_y + core, 2 * chip_d + core
        zlow, zhigh = lax.rem(z, 2), z // 2
        zdelta = (1 - 2 * zlow, 2 * (1 - 2 * zhigh))
        zpeers = (z + zdelta[0], z + zdelta[1], z + zdelta[0] + zdelta[1])
        zslab = (z,) + zpeers
        tlow, tmid, thigh = core, xbit, ybit

        def lanes(block):
            return pl.ds(pl.multiple_of(block * LANES, LANES), LANES)

        def rows_at(start, size):
            return pl.ds(pl.multiple_of(start, 16), size)

        def local(i, source, target):
            return pltpu.make_async_copy(source, target, b["local"].at[i])

        def landing(n, size):
            return act.at[pl.ds(0, size), n * LANES : (n + 1) * LANES]

        conv_in, out_in = landing(0, 256), landing(1, 128)
        cond_in, table_in = b["cond_in"], b["table_in"]
        small = [
            local(0, conv_w, conv_in),
            local(1, out_w, out_in),
            local(2, cond_w, cond_in),
            local(3, table_w, table_in),
        ]
        large = [
            local(4, audio.at[0], taps.at[1]),
            local(5, conditioning.at[0], cn),
            local(6, grad_res.at[0], agrad),
            local(7, grad_skip.at[0], skip),
        ]
        for copy in small:
            copy.start()

        barrier = pltpu.get_barrier_semaphore()
        peers = []
        for k in range(1, 32):
            pt = t
            for bit, step in ((tlow, 1), (tmid, 2), (thigh, 4)):
                if k & step:
                    pt = pt + step * (1 - 2 * bit)
            peers.append((pt, zslab[k >> 3]))
        near = [peer for k, peer in enumerate(peers, 1) if k < 8 or k % 8 == 0]
        for peer in near:
            pl.semaphore_signal(barrier, inc=1, device_id=peer, device_id_type=MESH)
        for copy in large:
            copy.start()

        for copy in small:
            copy.wait()
        wall[z, 0:256, lanes(t)] = conv_in[...].astype(BF16)
        wo[z, :, lanes(t)] = out_in[...].astype(BF16)
        pad_c = jnp.zeros((self.table_at - self.cond_rows, LANES), F32)
        pad_t = jnp.zeros((self.misc_rows - self.table_at - self.table_rows, LANES), F32)
        wall[z, 256 : self.BLOCK_ROWS, lanes(t)] = jnp.concatenate(
            [cond_in[...], pad_c, table_in[...], pad_t], axis=0
        ).astype(BF16)
        pl.semaphore_wait(barrier, len(near))

        def slab(weight, d, block):
            if weight == 2:
                return wo.at[pl.ds(zslab[d], 1), :, lanes(block)]
            row, size = self.PARTS[weight]
            return wall.at[pl.ds(zslab[d], 1), pl.ds(row, size), lanes(block)]

        def g_copy(unit, block, d, where, arrival):
            ref = slab(unit, d, block)
            return pltpu.make_async_remote_copy(
                src_ref=ref,
                dst_ref=ref,
                send_sem=b["sent"].at[unit // 2],
                recv_sem=b["g_recv"].at[arrival],
                device_id=where,
                device_id_type=MESH,
            )

        def g_of(unit, kind, d):
            if kind == "z":
                return g_copy(unit, t, 0, (t, zslab[d]), 3 * unit + d - 1 if unit < 2 else 6)
            if kind in "xyf":
                n = "xyf".index(kind)
                block, where = (
                    ((t, (tx, z)), (t, (ty, z)))[n] if n < 2 else ((tx, (ty, z)), (ty, (tx, z)))[d % 2]
                )
                return g_copy(unit, block, d, where, 7 + 8 * n + 4 * unit + d if unit < 2 else 31 + n)
            column = int(kind[1])
            arrival = 34 + 2 * column + d // 2 if unit < 2 else 42
            return g_copy(unit, (t, tx, ty, td)[column], d, (sib, z), arrival)

        def g_start(unit, d, *kinds):
            for kind in kinds:
                g_of(unit, kind, d).start()

        def g_z(unit, d):
            g_of(unit, "z", d).wait_recv()
            g_start(unit, d, "x", "y", "c0")

        def g_xy(unit, d):
            g_of(unit, "x", d).wait_recv()
            g_start(unit, d, *(("f", "c1") if d % 2 == 0 else ("c1",)))
            g_of(unit, "y", d).wait_recv()
            g_start(unit, d, *(("f", "c2") if d % 2 == 1 else ("c2",)))

        def g_d(unit, d):
            g_of(unit, "f", d).wait_recv()
            g_start(unit, d, "c3")

        def arrived(ref, sem):
            pltpu.make_async_remote_copy(
                src_ref=ref,
                dst_ref=ref,
                send_sem=b["sent"].at[0],
                recv_sem=sem,
                device_id=(sib, z),
                device_id_type=MESH,
            ).wait_recv()

        def g_core(column, far):
            pair = 2 * zhigh if far == 0 else 2 - 2 * zhigh
            block = (sib, 2 * chip_x + 1 - core, 2 * chip_y + 1 - core, 2 * chip_d + 1 - core)[column]
            ref = wall.at[pl.ds(pair, 2), :, lanes(block)]
            arrived(ref, b["g_recv"].at[34 + 2 * column + far])

        def o_first():
            for d in (1, 2, 3):
                g_start(2, d, "z")

        def o_xy():
            arrived(wo.at[0:3, :, lanes(t)], b["g_recv"].at[6])
            for d in range(4):
                g_start(2, d, "x", "y", "c0")

        def o_f():
            arrived(wo.at[:, :, lanes(tx)], b["g_recv"].at[31])
            arrived(wo.at[:, :, lanes(ty)], b["g_recv"].at[32])
            for d in range(4):
                g_start(2, d, "f", "c1", "c2")

        def o_d():
            arrived(wo.at[:, :, lanes(td)], b["g_recv"].at[33])
            for d in range(4):
                g_start(2, d, "c3")

        def o_core():
            arrived(wo.at[:, :, 0 : 4 * LANES], b["g_recv"].at[42])

        def halo_in():
            return pltpu.make_async_remote_copy(
                src_ref=audio.at[0, pl.ds(steps - DILATION_SIZE, DILATION_SIZE), :],
                dst_ref=b["halo"],
                send_sem=b["sent"].at[2],
                recv_sem=b["h_recv"].at[0],
                device_id=(jnp.minimum(t + 1, 7), z),
                device_id_type=MESH,
            )

        def halo_back():
            return pltpu.make_async_remote_copy(
                src_ref=b["phs"],
                dst_ref=b["phr"],
                send_sem=b["sent"].at[3],
                recv_sem=b["h_recv"].at[1],
                device_id=(jnp.maximum(t - 1, 0), z),
                device_id_type=MESH,
            )

        def loop(count, body):
            lax.fori_loop(0, count, lambda i, c: (body(i), c)[1], 0)

        def make_mask():
            cut = 1024
            spread = jnp.where(lax.broadcasted_iota(jnp.int32, (16, LANES), 0) == 0, 1.0, 0.0)
            for c in range(steps // cut):
                p = t * steps + c * cut + lax.broadcasted_iota(jnp.int32, (16, cut), 1)
                drop = None
                for j in range(self.seg_count):
                    d = p - starts[0, j]
                    hit = (d >= 0) & (d < DILATION_SIZE)
                    drop = hit if drop is None else drop | hit
                keep = jnp.where(drop, 0.0, 1.0).astype(BF16)
                km[c * cut : (c + 1) * cut, :] = dot_tn(keep, spread.astype(BF16)).astype(BF16)

        def make_extra():
            cut = 1024
            n = self.misc_rows
            for c in range(steps // cut):
                at = pl.ds(c * cut, cut)
                p = t * steps + c * cut + lax.broadcasted_iota(jnp.int32, (1, cut), 1)
                speaker = jnp.full((1, cut), ids[0, 0], jnp.int32)
                for j in range(1, self.seg_count):
                    speaker = jnp.where(p >= starts[0, j], ids[0, j], speaker)
                wide_speaker = jnp.broadcast_to(speaker, (n, cut))
                for q in range(4):
                    row = lax.broadcasted_iota(jnp.int32, (n, self.cond_dim), 0)
                    col = lax.broadcasted_iota(jnp.int32, (n, self.cond_dim), 1)
                    pick = (col == row + q * self.cond_rows) & (row < self.cond_rows)
                    pick = jnp.where(pick, 1.0, 0.0).astype(BF16)
                    mel = dot_nn(pick, cn[:, at])
                    slot = lax.broadcasted_iota(jnp.int32, (n, cut), 0) - self.table_at
                    ours = (slot >= 0) & (slot < self.table_rows)
                    hot = ours & (slot + q * self.table_rows == wide_speaker)
                    part = jnp.where(hot, 1.0, mel)
                    et[q * n : (q + 1) * n, at] = part.astype(BF16)

        def flip_extra():
            cut = 1024
            for c in range(steps // cut):
                at = pl.ds(c * cut, cut)
                extra[at, :] = et[:, at].T

        def make_prev():
            def shift(at, value):
                keep = jnp.concatenate([km[at, :]] * (ch // LANES), axis=1)
                taps[0, at, :] = value * keep

            shift(pl.ds(0, DILATION_SIZE), b["halo"][...])
            size = (steps - DILATION_SIZE) // 4

            def body(i):
                at = rows_at(i * size, size)
                shift(rows_at(i * size + DILATION_SIZE, size), taps[1, at, :])

            loop(4, body)

        def mixture_first(block):
            size = steps // 2
            cols = pl.ds(pl.multiple_of(256 * block, 256), 256)

            def body(i):
                at = rows_at(i * size, size)
                w = wall[pl.ds(2 * zhigh, 2), 0:256, cols].reshape(ch, 256)
                act[at, cols] = dot_nn(taps[zhigh, at, :], w)

            loop(2, body)

        def mixture(block, other=None):
            size = steps // 2
            cols = pl.ds(pl.multiple_of(256 * block, 256), 256)
            is_gate = block // 2
            scale = jnp.where(is_gate == 1, 0.5, 1.0).astype(F32)
            c0 = pl.ds(pl.multiple_of(256 * lax.rem(block, 2), 256), 256)

            def body(i):
                at = rows_at(i * size, size)
                w = wall[pl.ds(2 - 2 * zhigh, 2), 0:256, cols].reshape(ch, 256)
                m = wall[:, 256 : self.BLOCK_ROWS, cols].reshape(4 * self.misc_rows, 256)
                x = act[at, cols] + dot_nn(taps[1 - zhigh, at, :], w) + dot_nn(extra[at, :], m)
                x = scale * jnp.tanh(scale * x) + (1.0 - scale)
                act[at, cols] = x
                if other is not None:
                    y = act[at, pl.ds(pl.multiple_of(256 * other, 256), 256)]
                    gated[at, c0] = (x * y).astype(BF16)

            loop(2, body)

        def mixture_grad(half):
            size = 512
            w = wo[...].reshape(ch, 2 * ch)
            for i in range(half * 3, half * 3 + 3):
                at = pl.ds(i * size, size)
                q = dot_nt(agrad[at, :], w[:, :ch]) + dot_nt(skip[at, :], w[:, ch:])
                th, sg = act[at, :ch], act[at, ch:]
                g = th * sg
                mg[at, :ch] = (q * (sg - g * th)).astype(BF16)
                mg[at, ch:] = (q * (g - g * sg)).astype(BF16)

        def wtaps(first):
            return wall[first : first + 2, 0:256, :].reshape(ch, 2 * ch)

        def head_back():
            at = pl.ds(0, DILATION_SIZE)
            keep = jnp.concatenate([km[at, :].astype(F32)] * (ch // LANES), axis=1)
            b["phs"][...] = (keep * dot_nt(mg[at, :], wtaps(0))).astype(BF16)

            @pl.when(t > 0)
            def _():
                halo_back().start()

        def own_ref(j):
            return (own, self.CHUNK * j) if j < 2 else (act, self.CHUNK * (j - 2))

        def store_grad(j, value):
            at = pl.ds(self.CHUNK * j, self.CHUNK)
            keep, row = own_ref(j)
            even = core == 0
            for k in range(4):
                left = value[:, 2 * k * LANES : (2 * k + 1) * LANES]
                right = value[:, (2 * k + 1) * LANES : (2 * k + 2) * LANES]
                cols = slice(k * LANES, (k + 1) * LANES)
                keep[pl.ds(row, self.CHUNK), cols] = jnp.where(even, left, right)
                b["ss"][at, cols] = jnp.where(even, right, left).astype(BF16)

        def conv_grad(part):
            side, h = part % 2, part // 2
            lo = slice(h * 128, h * 128 + 128)
            hi = slice(256 + h * 128, 256 + h * 128 + 128)
            lhs = jnp.concatenate([taps[side, :, lo], taps[side, :, hi]], axis=1)
            store_grad(2 + part, dot_tn(lhs, mg[...]))

        def misc_grad():
            store_grad(6, dot_nn(et[...], mg[...]))

        def out_grad(part):
            lhs = gated[:, 256 * part : 256 * (part + 1)]
            value = jnp.concatenate([dot_tn(lhs, agrad[...]), dot_tn(lhs, skip[...])], axis=1)
            store_grad(part, value)

        def projected(which, i):
            size = steps // 2
            cols = slice(which * ch, (which + 1) * ch)
            at = pl.ds(i * size, size)
            value = dot_nn(gated[at, :], wo[:, :, cols].reshape(ch, ch))
            if which == 0:
                value = value + taps[1, at, :].astype(F32)
            (res, skip)[which][at, :] = value.astype(BF16)

        def audio_block(at, later):
            keep = jnp.concatenate([km[later, :].astype(F32)] * (ch // LANES), axis=1)
            total = agrad[at, :].astype(F32) + dot_nt(mg[at, :], wtaps(2))
            agrad[at, :] = (total + keep * dot_nt(mg[later, :], wtaps(0))).astype(BF16)

        def audio_main(i):
            size = (steps - DILATION_SIZE) // 4
            audio_block(pl.ds(i * size, size), pl.ds(i * size + DILATION_SIZE, size))

        def audio_last():
            @pl.when(t < 7)
            def _():
                halo_back().wait_recv()

            @pl.when(t == 7)
            def _():
                b["phr"][...] = jnp.zeros((DILATION_SIZE, ch), BF16)

            at = pl.ds(steps - DILATION_SIZE, DILATION_SIZE)
            total = agrad[at, :].astype(F32) + dot_nt(mg[at, :], wtaps(2))
            agrad[at, :] = (total + b["phr"][...].astype(F32)).astype(BF16)

        def r_copy(j, source, target, where, arrival):
            return pltpu.make_async_remote_copy(
                src_ref=source,
                dst_ref=target,
                send_sem=b["sent"].at[4 + arrival // 2],
                recv_sem=b["r_recv"].at[j, arrival],
                device_id=where,
                device_id_type=MESH,
            )

        def r_start(*args):
            r_copy(*args).start()

        def r_arrived(j, ref, arrival):
            r_copy(j, ref, ref, (sib, z), arrival).wait_recv()

        def part_rows(j, start, size):
            return rows_at(self.CHUNK * j + start, size)

        def pair_sum(j, start, size, block):
            ref, row = own_ref(j)
            other = b["sr"][part_rows(j, start, size), lanes(block)].astype(F32)
            return ref[rows_at(row + start, size), lanes(block)] + other

        def r_s(j):
            at = pl.ds(self.CHUNK * j, self.CHUNK)
            r_start(j, b["ss"].at[at, :], b["sr"].at[at, :], (sib, z), 0)

        def r_1(j):
            row, half = self.CHUNK * j, self.CHUNK // 2
            r_arrived(j, b["sr"].at[pl.ds(row, self.CHUNK), :], 0)
            at = pl.ds(row // 2, half)
            for i, where in enumerate(((tx, z), (ty, z))):
                b["r1s"][i, at, :] = pair_sum(j, i * half, half, chip_d).astype(BF16)
                r_start(j, b["r1s"].at[i, at, :], b["r1r"].at[i, at, :], where, 1)

        def r_3(j):
            row, half = self.CHUNK * j, self.CHUNK // 2
            up, low = pl.ds(row, half), pl.ds(row + half, half)
            at, every = pl.ds(row // 2, half), pl.ds(row, self.CHUNK)
            b["r3s"][0, up, :] = pair_sum(j, 0, half, chip_x).astype(BF16)
            b["r3s"][1, low, :] = pair_sum(j, half, half, chip_y).astype(BF16)
            r_arrived(j, b["r1r"].at[:, at, :], 1)
            b["r3s"][0, low, :] = (
                pair_sum(j, half, half, chip_x) + b["r1r"][1, at, :].astype(F32)
            ).astype(BF16)
            r_start(j, b["r3s"].at[0, every, :], b["r3r"].at[0, every, :], (tx, z), 2)
            b["r3s"][1, up, :] = (
                pair_sum(j, 0, half, chip_y) + b["r1r"][0, at, :].astype(F32)
            ).astype(BF16)
            r_start(j, b["r3s"].at[1, every, :], b["r3r"].at[1, every, :], (ty, z), 2)

        def plane_sum(j, start, size):
            at = part_rows(j, start, size)
            return (
                pair_sum(j, start, size, chip)
                + b["r3r"][0, at, :].astype(F32)
                + b["r3r"][1, at, :].astype(F32)
            )

        def final(j):
            if j < 2:
                return fout
            return fconv.at[pl.ds(128 * ((j - 2) // 2), 128), :] if j < 6 else fmisc

        def z_rows(j):
            return 64 if self.PAIRS[j] is None else 128

        def z_at(j, which):
            place = which if self.PAIRS[j] is None else lax.rem(which, 2)
            return place * z_rows(j)

        def z_copy(j, d):
            at = pl.ds(128 * (j // 2), z_rows(j))
            return r_copy(
                j, b["zs"].at[part_rows(j, z_at(j, zslab[d]), z_rows(j)), :], b["zr"].at[d - 1, at, :], (t, zslab[d]), 3
            )

        def r_z(j):
            every = pl.ds(self.CHUNK * j, self.CHUNK)
            r_arrived(j, b["r3r"].at[:, every, :], 2)
            b["zs"][every, :] = plane_sum(j, 0, self.CHUNK).astype(BF16)
            if self.PAIRS[j] is None:
                for d in (1, 2, 3):
                    z_copy(j, d).start()
                final(j)[...] = plane_sum(j, z_at(j, z), z_rows(j))
                return
            ours = zhigh == self.PAIRS[j]

            @pl.when(ours)
            def _():
                z_copy(j, 1).start()
                final(j)[...] = plane_sum(j, z_at(j, z), z_rows(j))

            @pl.when(jnp.logical_not(ours))
            def _():
                z_copy(j, 2).start()
                z_copy(j, 3).start()

        def r_f(j):
            def add():
                at = pl.ds(128 * (j // 2), z_rows(j))
                r_arrived(j, b["zr"].at[:, at, :], 3)
                total = final(j)[...]
                for i in range(3):
                    total = total + b["zr"][i, at, :].astype(F32)
                final(j)[...] = total

            if self.PAIRS[j] is None:
                add()
            else:
                pl.when(zhigh == self.PAIRS[j])(add)

        def n_copy(peer):
            mine = b["squares"].at[4 * t + z]
            return pltpu.make_async_remote_copy(
                src_ref=mine,
                dst_ref=mine,
                send_sem=b["sent"].at[6],
                recv_sem=b["n_recv"],
                device_id=peer,
                device_id_type=MESH,
            )

        def norm_start():
            total = jnp.zeros((8, LANES), F32)
            for ref in (fconv, fmisc, fout):
                value = ref[...]
                total = total + jnp.sum((value * value).reshape(-1, 8, LANES), axis=0)
            b["squares"][4 * t + z] = jnp.sum(total, axis=0, keepdims=True)
            for peer in peers:
                n_copy(peer).start()

        def norm_end():
            arrived(b["squares"].at[0:31], b["n_recv"])
            norm[...] = jnp.sum(b["squares"][...], axis=0)

        for unit in (0, 1):
            for d in (1, 2, 3):
                g_start(unit, d, "z")
            g_start(unit, 0, "x", "y", "c0")

        @pl.when(t < 7)
        def _():
            halo_in().start()

        make_mask()
        large[1].wait()
        make_extra()
        flip_extra()
        g_xy(0, 0)
        g_z(0, 1)
        g_xy(1, 0)
        g_z(1, 1)
        large[0].wait()

        @pl.when(t == 0)
        def _():
            b["halo"][...] = jnp.zeros((DILATION_SIZE, ch), BF16)

        @pl.when(t > 0)
        def _():
            halo_in().wait_recv()

        make_prev()
        g_z(0, 2)
        g_z(1, 2)
        g_core(0, 0)
        mixture_first(chip)
        g_xy(0, 1)
        g_d(0, 0)
        g_xy(1, 1)
        g_d(1, 0)
        g_z(0, 3)
        g_z(1, 3)
        o_first()
        g_core(2, 0)
        mixture_first(chip_y)
        g_xy(0, 2)
        g_xy(1, 2)
        g_d(0, 1)
        g_d(1, 1)
        g_core(1, 0)
        mixture_first(chip_x)
        g_xy(0, 3)
        g_xy(1, 3)
        o_xy()
        g_core(0, 1)
        mixture(chip)
        g_d(0, 2)
        g_d(1, 2)
        g_core(3, 0)
        mixture_first(chip_d)
        g_d(0, 3)
        g_d(1, 3)
        g_core(2, 1)
        mixture(chip_y, chip)
        g_core(1, 1)
        mixture(chip_x)
        o_f()
        g_core(3, 1)
        mixture(chip_d, chip_x)
        large[2].wait()
        large[3].wait()
        out_grad(0)
        r_s(0)
        o_d()
        out_grad(1)
        r_s(1)
        r_1(0)
        o_core()
        mixture_grad(0)
        r_1(1)
        r_3(0)
        mixture_grad(1)
        head_back()
        misc_grad()
        r_s(6)
        r_3(1)
        conv_grad(0)
        r_s(2)
        r_1(6)
        r_z(0)
        conv_grad(1)
        r_s(3)
        r_z(1)
        r_1(2)
        r_3(6)
        conv_grad(2)
        r_s(4)
        r_1(3)
        r_3(2)
        r_f(0)
        conv_grad(3)
        r_s(5)
        r_z(6)
        r_1(4)
        r_3(3)
        r_f(1)
        audio_main(0)
        r_1(5)
        r_z(2)
        r_3(4)
        audio_main(1)
        r_f(6)
        r_z(3)
        r_3(5)
        audio_main(2)
        r_f(2)
        audio_main(3)
        r_z(4)
        r_f(3)
        r_z(5)
        projected(0, 0)
        projected(0, 1)
        r_f(4)
        r_f(5)
        norm_start()
        projected(1, 0)
        projected(1, 1)
        audio_last()
        norm_end()

        def left(i, ref):
            pltpu.make_async_remote_copy(
                src_ref=ref,
                dst_ref=ref,
                send_sem=b["sent"].at[i],
                recv_sem=b["n_recv"],
                device_id=(sib, z),
                device_id_type=MESH,
            ).wait_send()

        row = 2 * ch
        wall_bytes = 31 * 2 * self.BLOCK_ROWS * LANES
        wo_bytes = 31 * 2 * 128 * LANES
        part_bytes = 2 * self.CHUNK * LANES
        parts = len(self.PAIRS)
        early = parts * (4 + 1) * part_bytes
        late = parts * 2 * part_bytes + 9 * part_bytes // 2 + 3 * part_bytes // 4
        for i, count in ((0, wall_bytes), (1, wo_bytes), (4, early), (5, late)):
            left(i, taps.at[0, pl.ds(0, count // row), :])
        left(6, b["squares"].at[0:31])

        @pl.when(t < 7)
        def _():
            halo_in().wait_send()

        @pl.when(t > 0)
        def _():
            halo_back().wait_send()

    def __call__(self, ids, starts, audio, conditioning, grad_res, grad_skip, conv_w, cond_w, table_w, out_w):
        steps, ch = self.steps, self.channels
        wide = pltpu.VMEM((steps, ch), BF16)
        smem = pl.BlockSpec(memory_space=pltpu.SMEM)
        anywhere = pl.BlockSpec(memory_space=pl.ANY)
        vmem = pl.BlockSpec(memory_space=pltpu.VMEM)
        return pl.pallas_call(
            self.kernel,
            out_shape=[
                wide,
                wide,
                wide,
                pltpu.VMEM((256, LANES), F32),
                pltpu.VMEM((self.misc_rows, LANES), F32),
                pltpu.VMEM((128, LANES), F32),
                pltpu.VMEM((1, LANES), F32),
            ],
            in_specs=[smem, smem] + [anywhere] * 8,
            out_specs=[vmem] * 7,
            scratch_shapes=list(self.scratch().values()),
            compiler_params=pltpu.CompilerParams(
                collective_id=0, has_side_effects=True, vmem_limit_bytes=54 * 2**20
            ),
            name="layer",
        )(ids, starts, audio, conditioning, grad_res, grad_skip, conv_w, cond_w, table_w, out_w)


def closing_kernel(cond_rows, table_at, table_rows, *refs):
    (res, skip, agrad, fconv, fmisc, fout, norm), refs = refs[:7], refs[7:]
    state, refs = refs[:12], refs[12:]
    (res_o, skip_o, agrad_o, prenorm_o), refs = refs[:4], refs[4:]
    new, (sems,) = refs[:12], refs[12:]
    copies = [
        pltpu.make_async_copy(source, target.at[0], sems.at[i])
        for i, (source, target) in enumerate(((res, res_o), (skip, skip_o), (agrad, agrad_o)))
    ]
    for copy in copies:
        copy.start()
    prenorm = jnp.sqrt(jnp.sum(norm[...], keepdims=True))
    prenorm_o[...] = prenorm
    factor = jnp.minimum(1.0, clip_level / (prenorm + 1e-06))
    grads = (
        fconv[...],
        fmisc[0:cond_rows, :],
        fmisc[table_at : table_at + table_rows, :],
        fout[...],
    )
    for k, grad in enumerate(grads):
        master, first, second = (state[3 * k + i][...] for i in range(3))
        for i, value in enumerate(adamw(grad, factor, master, first, second)):
            new[3 * k + i][...] = value
    for copy in copies:
        copy.wait()


def closing(layer, results, state):
    wide = jax.ShapeDtypeStruct((1, layer.steps, layer.channels), BF16)
    vmem = pl.BlockSpec(memory_space=pltpu.VMEM)
    anywhere = pl.BlockSpec(memory_space=pl.ANY)
    return pl.pallas_call(
        functools.partial(closing_kernel, layer.cond_rows, layer.table_at, layer.table_rows),
        out_shape=[wide, wide, wide, jax.ShapeDtypeStruct((1, 1), F32)]
        + [jax.ShapeDtypeStruct(a.shape, F32) for a in state],
        in_specs=[vmem] * 19,
        out_specs=[anywhere] * 3 + [vmem] * 13,
        scratch_shapes=[pltpu.SemaphoreType.DMA((3,))],
        compiler_params=pltpu.CompilerParams(vmem_limit_bytes=32 * 2**20),
        name="closing",
    )(*results, *state)


def on_device_kernels(
    audio,
    conditioning,
    speaker_ids,
    seg_starts,
    grad_residual,
    grad_skip,
    conv_weight,
    conv_first,
    conv_second,
    cond_weight,
    cond_first,
    cond_second,
    speaker_table,
    table_first,
    table_second,
    out_weight,
    out_first,
    out_second,
):
    layer = Layer(
        audio.shape[1],
        audio.shape[2],
        conditioning.shape[1],
        cond_weight.shape[0],
        speaker_table.shape[0],
        seg_starts.shape[1],
    )
    results = layer(
        speaker_ids,
        seg_starts,
        audio,
        conditioning,
        grad_residual,
        grad_skip,
        conv_weight,
        cond_weight,
        speaker_table,
        out_weight,
    )
    state = (
        conv_weight,
        conv_first,
        conv_second,
        cond_weight,
        cond_first,
        cond_second,
        speaker_table,
        table_first,
        table_second,
        out_weight,
        out_first,
        out_second,
    )
    done = closing(layer, results, state)
    return (done[0], done[1], done[2], done[3].reshape(()), *done[4:])


def passed_along(value, axis, steps):
    count = lax.axis_size(axis)
    first, last = (max(0, -steps), min(count, count - steps))
    return lax.ppermute(value, axis, [(source, source + steps) for source in range(first, last)])


def contract_rows(left, right):
    return lax.dot_general(
        left, right, (((0,), (0,)), ((), ())), preferred_element_type=jnp.float32
    )


def contract_cols(left, right):
    return lax.dot_general(
        left, right, (((1,), (1,)), ((), ())), preferred_element_type=jnp.float32
    )


def own_block(whole, shard):
    row_start = lax.axis_index("batch") * shard.shape[0]
    col_start = lax.axis_index("tm") * shard.shape[1]
    return lax.dynamic_slice(whole, (row_start, col_start), shard.shape)


def square_sum(matrix):
    return jnp.sum(matrix * matrix)


def on_device(
    audio,
    conditioning,
    speaker_ids,
    seg_starts,
    grad_residual,
    grad_skip,
    conv_weight,
    conv_first,
    conv_second,
    cond_weight,
    cond_first,
    cond_second,
    speaker_table,
    table_first,
    table_second,
    out_weight,
    out_first,
    out_second,
):
    rows_dev, steps_per_device, channels = audio.shape
    tokens = rows_dev * steps_per_device
    conv_rows, cond_rows, table_rows, out_rows = (
        lax.all_gather(conv_weight.astype(jnp.bfloat16), "batch", axis=0, tiled=True),
        lax.all_gather(cond_weight.astype(jnp.bfloat16), "batch", axis=0, tiled=True),
        lax.all_gather(speaker_table.astype(jnp.bfloat16), "batch", axis=0, tiled=True),
        lax.all_gather(out_weight.astype(jnp.bfloat16), "batch", axis=0, tiled=True),
    )
    conv_full, cond_full, table_full, out_full = (
        lax.all_gather(conv_rows, "tm", axis=1, tiled=True),
        lax.all_gather(cond_rows, "tm", axis=1, tiled=True),
        lax.all_gather(table_rows, "tm", axis=1, tiled=True),
        lax.all_gather(out_rows, "tm", axis=1, tiled=True),
    )
    offset = lax.axis_index("tm") * steps_per_device
    positions = offset + jnp.arange(steps_per_device, dtype=jnp.int32)
    seg_count = seg_starts.shape[1]
    segment = (
        jnp.sum((positions[None, :, None] >= seg_starts[:, None, :]).astype(jnp.int32), axis=2) - 1
    )
    seg_match = segment[:, :, None] == jnp.arange(seg_count, dtype=jnp.int32)[None, None, :]
    local_start = jnp.sum(jnp.where(seg_match, seg_starts[:, None, :], 0), axis=2)
    retain_mask = (positions[None, :] - DILATION_SIZE >= local_start).astype(jnp.bfloat16)
    seg_hot = seg_match.astype(jnp.bfloat16)
    speakers = table_full.shape[0]
    speaker_hot = (
        speaker_ids[:, :, None] == jnp.arange(speakers, dtype=jnp.int32)[None, None, :]
    ).astype(jnp.bfloat16)
    seg_embed = jnp.einsum(
        "rsk,kf->rsf", speaker_hot, table_full, preferred_element_type=jnp.float32
    ).astype(jnp.bfloat16)
    tail_input = passed_along(audio[:, steps_per_device - DILATION_SIZE :, :], "tm", 1)
    previous = (
        jnp.concatenate([tail_input, audio[:, : steps_per_device - DILATION_SIZE, :]], axis=1)
        * retain_mask[:, :, None]
    )
    flat_audio = audio.reshape(tokens, channels)
    flat_prev = previous.reshape(tokens, channels)
    mixture = jnp.dot(flat_prev, conv_full[:channels], preferred_element_type=jnp.float32)
    mixture = mixture + jnp.dot(
        flat_audio, conv_full[channels:], preferred_element_type=jnp.float32
    )
    mixture = mixture + jnp.einsum(
        "rct,cf->rtf", conditioning, cond_full, preferred_element_type=jnp.float32
    ).reshape(tokens, -1)
    mixture = mixture + jnp.einsum(
        "rts,rsf->rtf", seg_hot, seg_embed, preferred_element_type=jnp.float32
    ).reshape(tokens, -1)
    filter_tanh = jnp.tanh(mixture[:, :channels])
    gate_sig = jax.nn.sigmoid(mixture[:, channels:])
    gated_out = (filter_tanh * gate_sig).astype(jnp.bfloat16)
    projected = jnp.dot(gated_out, out_full, preferred_element_type=jnp.float32)
    residual_out = (
        (flat_audio.astype(jnp.float32) + projected[:, :channels])
        .astype(jnp.bfloat16)
        .reshape(audio.shape)
    )
    skip_out = projected[:, channels:].astype(jnp.bfloat16).reshape(audio.shape)
    back_out = jnp.concatenate(
        [grad_residual.reshape(tokens, channels), grad_skip.reshape(tokens, channels)], axis=1
    )
    out_grad = contract_rows(gated_out, back_out)
    gated_grad = contract_cols(back_out, out_full)
    filter_grad = gated_grad * gate_sig * (1.0 - filter_tanh * filter_tanh)
    gate_grad = gated_grad * filter_tanh * gate_sig * (1.0 - gate_sig)
    mixture_grad = jnp.concatenate([filter_grad, gate_grad], axis=1).astype(jnp.bfloat16)
    conv_grad = jnp.concatenate(
        [contract_rows(flat_prev, mixture_grad), contract_rows(flat_audio, mixture_grad)], axis=0
    )
    grad_blocks = mixture_grad.reshape(rows_dev, steps_per_device, -1)
    cond_grad = jnp.einsum(
        "rct,rtf->cf", conditioning, grad_blocks, preferred_element_type=jnp.float32
    )
    seg_sums = jnp.einsum("rts,rtf->rsf", seg_hot, grad_blocks, preferred_element_type=jnp.float32)
    table_grad = jnp.einsum(
        "rsk,rsf->kf",
        speaker_hot.astype(jnp.float32),
        seg_sums,
        precision=lax.Precision.HIGHEST,
        preferred_element_type=jnp.float32,
    )
    preceding_gradient = (
        contract_cols(mixture_grad, conv_full[:channels]).reshape(audio.shape)
        * retain_mask[:, :, None]
    ).astype(jnp.bfloat16)
    head_input = passed_along(preceding_gradient[:, :DILATION_SIZE, :], "tm", -1)
    later_contribution = jnp.concatenate(
        [preceding_gradient[:, DILATION_SIZE:, :], head_input], axis=1
    ).astype(jnp.float32)
    current_tap = contract_cols(mixture_grad, conv_full[channels:]).reshape(audio.shape)
    audio_grad = (grad_residual.astype(jnp.float32) + current_tap + later_contribution).astype(
        jnp.bfloat16
    )
    conv_total, cond_total, table_total, out_total = lax.psum(
        (conv_grad, cond_grad, table_grad, out_grad), ("tm", "batch")
    )
    squares = (
        square_sum(conv_total)
        + square_sum(cond_total)
        + square_sum(table_total)
        + square_sum(out_total)
    )
    conv_part = own_block(conv_total, conv_weight)
    cond_part = own_block(cond_total, cond_weight)
    table_part = own_block(table_total, speaker_table)
    out_part = own_block(out_total, out_weight)
    prenorm = jnp.sqrt(squares)
    factor = jnp.minimum(1.0, clip_level / (prenorm + 1e-06))
    conv_state = adamw(conv_part, factor, conv_weight, conv_first, conv_second)
    cond_state = adamw(cond_part, factor, cond_weight, cond_first, cond_second)
    table_state = adamw(table_part, factor, speaker_table, table_first, table_second)
    out_state = adamw(out_part, factor, out_weight, out_first, out_second)
    return (
        residual_out,
        skip_out,
        audio_grad,
        prenorm,
        conv_state[0],
        conv_state[1],
        conv_state[2],
        cond_state[0],
        cond_state[1],
        cond_state[2],
        table_state[0],
        table_state[1],
        table_state[2],
        out_state[0],
        out_state[1],
        out_state[2],
    )


def solution(mesh):
    placed = (
        P("batch", "tm", None),
        P("batch", None, "tm"),
        P("batch", None),
        P("batch", None),
        P("batch", "tm", None),
        P("batch", "tm", None),
        P("batch", "tm"),
        P("batch", "tm"),
        P("batch", "tm"),
        P("batch", "tm"),
        P("batch", "tm"),
        P("batch", "tm"),
        P("batch", "tm"),
        P("batch", "tm"),
        P("batch", "tm"),
        P("batch", "tm"),
        P("batch", "tm"),
        P("batch", "tm"),
    )
    small = mesh.shape["tm"] == 8 and mesh.shape["batch"] == 4
    return jax.shard_map(
        on_device_kernels if small else on_device,
        mesh=mesh,
        in_specs=placed,
        out_specs=(
            P("batch", "tm", None),
            P("batch", "tm", None),
            P("batch", "tm", None),
            P(),
            P("batch", "tm"),
            P("batch", "tm"),
            P("batch", "tm"),
            P("batch", "tm"),
            P("batch", "tm"),
            P("batch", "tm"),
            P("batch", "tm"),
            P("batch", "tm"),
            P("batch", "tm"),
            P("batch", "tm"),
            P("batch", "tm"),
            P("batch", "tm"),
        ),
        check_vma=False,
    )
```

```python
import functools

import jax
import jax.numpy as jnp
from jax import lax
from jax.experimental import pallas as pl
from jax.experimental.pallas import tpu as pltpu
from jax.sharding import PartitionSpec as P

DILATION_SIZE = 256
STEP = 10


clip_level = 1.0
beta_one = 0.9
beta_two = 0.999
adam_eps = 1e-08
decay_rate = 0.01
learn_rate = 0.1

LANES = 128
MESH = pl.DeviceIdType.MESH
BF16 = jnp.bfloat16
F32 = jnp.float32


def dot_nn(left, right):
    return lax.dot_general(left, right, (((1,), (0,)), ((), ())), preferred_element_type=F32)


def dot_nt(left, right):
    return lax.dot_general(left, right, (((1,), (1,)), ((), ())), preferred_element_type=F32)


def dot_tn(left, right):
    return lax.dot_general(left, right, (((0,), (0,)), ((), ())), preferred_element_type=F32)


def adamw(gradient, factor, master, first_old, second_old):
    clipped = gradient * factor
    new_first = beta_one * first_old + (1.0 - beta_one) * clipped
    new_second = beta_two * second_old + (1.0 - beta_two) * clipped * clipped
    step_size = (
        new_first
        / (1.0 - beta_one**STEP)
        / (jnp.sqrt(new_second / (1.0 - beta_two**STEP)) + adam_eps)
    )
    new_master = master - learn_rate * (step_size + decay_rate * master)
    return (new_first, new_second, new_master)


class Layer:
    def __init__(self, steps, channels, cond_dim, cond_rows, table_rows, seg_count):
        self.steps = steps
        self.channels = channels
        self.cond_dim = cond_dim
        self.cond_rows = cond_rows
        self.table_rows = table_rows
        self.seg_count = seg_count
        self.misc_rows = 64
        self.table_at = 32

    BLOCK_ROWS = 320
    PARTS = tuple((256 * j, 256, j % 2) for j in range(6)) + ((1536, 128, 0), (1664, 128, 1))
    GRAD_ROWS = 7 * 256

    def scratch(self):
        steps, ch = self.steps, self.channels
        wide = 2 * ch
        rows = self.GRAD_ROWS
        dma = pltpu.SemaphoreType.DMA
        return dict(
            taps=pltpu.VMEM((2, steps, ch), BF16),
            halo=pltpu.VMEM((DILATION_SIZE, ch), BF16),
            act=pltpu.VMEM((steps, wide), F32),
            own=pltpu.VMEM((512, 4 * LANES), F32),
            gated=pltpu.VMEM((steps, ch), BF16),
            mg=pltpu.VMEM((steps, wide), BF16),
            et=pltpu.VMEM((4 * self.misc_rows, steps), BF16),
            extra=pltpu.VMEM((steps, 4 * self.misc_rows), BF16),
            cn=pltpu.VMEM((self.cond_dim, steps), BF16),
            km=pltpu.VMEM((steps, LANES), BF16),
            wall=pltpu.VMEM((4, self.BLOCK_ROWS, wide), BF16),
            wo=pltpu.VMEM((4, 128, wide), BF16),
            ids=pltpu.SMEM((1, self.seg_count), jnp.int32),
            starts=pltpu.SMEM((1, self.seg_count), jnp.int32),
            cond_in=pltpu.VMEM((self.cond_rows, LANES), F32),
            table_in=pltpu.VMEM((self.table_rows, LANES), F32),
            ss=pltpu.VMEM((rows, 4 * LANES), BF16),
            sr=pltpu.VMEM((rows, 4 * LANES), BF16),
            r1s=pltpu.VMEM((2, rows // 2, LANES), BF16),
            r1r=pltpu.VMEM((2, rows // 2, LANES), BF16),
            r3s=pltpu.VMEM((2, rows, LANES), BF16),
            r3r=pltpu.VMEM((2, rows, LANES), BF16),
            zs=pltpu.VMEM((rows, LANES), BF16),
            zr=pltpu.VMEM((3, 4 * 128, LANES), BF16),
            phs=pltpu.VMEM((DILATION_SIZE, ch), BF16),
            phr=pltpu.VMEM((DILATION_SIZE, ch), BF16),
            squares=pltpu.VMEM((32, 1, LANES), F32),
            g_recv=dma((33,)),
            r_recv=dma((8, 4)),
            h_recv=dma((2,)),
            sent=dma((7,)),
            n_recv=dma,
            local=dma((10,)),
        )

    def kernel(
        self, ids_in, starts_in, audio, conditioning, grad_res, grad_skip, conv_w, cond_w, table_w, out_w, *rest
    ):
        names = list(self.scratch())
        outs, bufs = rest[: len(rest) - len(names)], rest[len(rest) - len(names) :]
        res, skip, agrad, fconv, fmisc, fout, norm = outs
        b = dict(zip(names, bufs))
        steps, ch = self.steps, self.channels
        taps, act, own, gated, mg = b["taps"], b["act"], b["own"], b["gated"], b["mg"]
        ids, starts = b["ids"], b["starts"]
        et, extra, cn, km, wall, wo = b["et"], b["extra"], b["cn"], b["km"], b["wall"], b["wo"]

        t = lax.axis_index("tm")
        z = lax.axis_index("batch")
        core = lax.rem(t, 2)
        chip = t // 2
        sib = t + 1 - 2 * core
        xbit = lax.rem(chip, 2)
        ybit = chip // 2
        xdelta = 1 - 2 * xbit
        ydelta = 2 * (1 - 2 * ybit)
        chip_x, chip_y, chip_d = chip + xdelta, chip + ydelta, chip + xdelta + ydelta
        tx, ty, td = 2 * chip_x + core, 2 * chip_y + core, 2 * chip_d + core
        zlow, zhigh = lax.rem(z, 2), z // 2
        zdelta = (1 - 2 * zlow, 2 * (1 - 2 * zhigh))
        zpeers = (z + zdelta[0], z + zdelta[1], z + zdelta[0] + zdelta[1])
        zslab = (z,) + zpeers
        tlow, tmid, thigh = core, xbit, ybit

        def lanes(block):
            return pl.ds(pl.multiple_of(block * LANES, LANES), LANES)

        def rows_at(start, size):
            return pl.ds(pl.multiple_of(start, 16), size)

        def local(i, source, target):
            return pltpu.make_async_copy(source, target, b["local"].at[i])

        def landing(n, size):
            return act.at[pl.ds(0, size), n * LANES : (n + 1) * LANES]

        conv_in, out_in = landing(0, 256), landing(1, 128)
        cond_in, table_in = b["cond_in"], b["table_in"]
        small = [
            local(0, conv_w, conv_in),
            local(1, out_w, out_in),
            local(2, cond_w, cond_in),
            local(3, table_w, table_in),
        ]
        large = [
            local(4, audio.at[0], taps.at[1]),
            local(5, conditioning.at[0], cn),
            local(6, grad_res.at[0], agrad),
            local(7, grad_skip.at[0], skip),
        ]
        scalars = [local(8, starts_in, starts), local(9, ids_in, ids)]
        for copy in small + scalars:
            copy.start()

        barrier = pltpu.get_barrier_semaphore()
        peers = []
        for k in range(1, 32):
            pt = t
            for bit, step in ((tlow, 1), (tmid, 2), (thigh, 4)):
                if k & step:
                    pt = pt + step * (1 - 2 * bit)
            peers.append((pt, zslab[k >> 3]))
        near = [peer for k, peer in enumerate(peers, 1) if k < 8 or k % 8 == 0]
        for peer in near:
            pl.semaphore_signal(barrier, inc=1, device_id=peer, device_id_type=MESH)
        for copy in large:
            copy.start()

        def barrier_wait():
            pl.semaphore_wait(barrier, len(near))

        for copy in small:
            copy.wait()
        wall[z, 0:256, lanes(t)] = conv_in[...].astype(BF16)
        wo[z, :, lanes(t)] = out_in[...].astype(BF16)
        pad_c = jnp.zeros((self.table_at - self.cond_rows, LANES), F32)
        pad_t = jnp.zeros((self.misc_rows - self.table_at - self.table_rows, LANES), F32)
        wall[z, 256 : self.BLOCK_ROWS, lanes(t)] = jnp.concatenate(
            [cond_in[...], pad_c, table_in[...], pad_t], axis=0
        ).astype(BF16)
        def slab(unit, e, block):
            d = min(e, 3)
            if unit == 1:
                return wo.at[pl.ds(zslab[d], 1), :, lanes(block)]
            size = self.BLOCK_ROWS if e < 3 else self.BLOCK_ROWS // 2
            return wall.at[pl.ds(zslab[d], 1), pl.ds(size if e == 4 else 0, size), lanes(block)]

        def g_copy(unit, ref, where, arrival):
            return pltpu.make_async_remote_copy(
                src_ref=ref,
                dst_ref=ref,
                send_sem=b["sent"].at[unit],
                recv_sem=b["g_recv"].at[arrival],
                device_id=where,
                device_id_type=MESH,
            )

        def g_of(unit, kind, e):
            if kind == "z":
                ref = slab(unit, 0, t)
                if unit == 0 and e >= 3:
                    size = self.BLOCK_ROWS // 2
                    ref = wall.at[pl.ds(z, 1), pl.ds((e - 3) * size, size), lanes(t)]
                return g_copy(unit, ref, (t, zslab[min(e, 3)]), 4 if unit else e - 1)
            if kind == "k":
                return g_copy(unit, slab(unit, 0, td), (t, zslab[1]), 16)
            if kind in "xyf":
                n = "xyf".index(kind)
                if kind == "f":
                    block, where = ((tx, (ty, z)), (ty, (tx, z)))[min(e, 3) % 2]
                else:
                    block, where = t, ((tx, z), (ty, z))[n]
                return g_copy(unit, slab(unit, e, block), where, 20 + n if unit else 5 + 5 * n + e)
            column = int(kind[1])
            arrival = 31 if unit else 23 + 2 * column + min(e, 3) // 2
            return g_copy(unit, slab(unit, e, (t, tx, ty, td)[column]), (sib, z), arrival)

        def g_start(unit, e, *kinds):
            for kind in kinds:
                g_of(unit, kind, e).start()

        def g_z(e):
            g_of(0, "z", e).wait_recv()
            g_start(0, e, "x", "y", "c0")

        def g_xy(e):
            g_of(0, "x", e).wait_recv()
            g_start(0, e, *(("f", "c1") if e in (0, 2) else ("c1",)))
            g_of(0, "y", e).wait_recv()
            g_start(0, e, *(("f", "c2") if e >= 3 else ("c2",)))

        def g_d(e):
            if e == 1:
                g_copy(0, slab(0, 1, td), (t, zslab[1]), 16).wait_recv()
            else:
                g_of(0, "f", e).wait_recv()
            g_start(0, e, *(("k", "c3") if e == 0 else ("c3",)))

        def arrived(ref, sem):
            pltpu.make_async_remote_copy(
                src_ref=ref,
                dst_ref=ref,
                send_sem=b["sent"].at[0],
                recv_sem=sem,
                device_id=(sib, z),
                device_id_type=MESH,
            ).wait_recv()

        def g_core(column, far):
            pair = 2 * zhigh if far == 0 else 2 - 2 * zhigh
            block = (sib, 2 * chip_x + 1 - core, 2 * chip_y + 1 - core, 2 * chip_d + 1 - core)[column]
            ref = wall.at[pl.ds(pair, 2), :, lanes(block)]
            arrived(ref, b["g_recv"].at[23 + 2 * column + far])

        def o_first():
            g_start(1, 0, "x", "y", "c0")

        def o_xy():
            g_of(1, "x", 0).wait_recv()
            g_start(1, 0, "f", "c1")
            g_of(1, "y", 0).wait_recv()
            g_start(1, 0, "c2")

        def o_z():
            g_of(1, "f", 0).wait_recv()
            g_start(1, 0, "c3")
            for d in (2, 3, 1):
                for block in (t, tx, ty, td):
                    g_copy(1, slab(1, 0, block), (t, zslab[d]), 4).start()

        def o_d():
            arrived(wo.at[0:3, :, 0 : 4 * LANES], b["g_recv"].at[4])
            for d in (1, 2, 3):
                g_start(1, d, "c0", "c1", "c2", "c3")

        def o_core():
            arrived(wo.at[:, :, 0 : 4 * LANES], b["g_recv"].at[31])

        def halo_in():
            return pltpu.make_async_remote_copy(
                src_ref=audio.at[0, pl.ds(steps - DILATION_SIZE, DILATION_SIZE), :],
                dst_ref=b["halo"],
                send_sem=b["sent"].at[2],
                recv_sem=b["h_recv"].at[0],
                device_id=(jnp.minimum(t + 1, 7), z),
                device_id_type=MESH,
            )

        def halo_back():
            return pltpu.make_async_remote_copy(
                src_ref=b["phs"],
                dst_ref=b["phr"],
                send_sem=b["sent"].at[3],
                recv_sem=b["h_recv"].at[1],
                device_id=(jnp.maximum(t - 1, 0), z),
                device_id_type=MESH,
            )

        def loop(count, body):
            lax.fori_loop(0, count, lambda i, c: (body(i), c)[1], 0)

        def make_mask():
            cut = 1024
            spread = jnp.where(lax.broadcasted_iota(jnp.int32, (16, LANES), 0) == 0, 1.0, 0.0)
            for c in range(steps // cut):
                p = t * steps + c * cut + lax.broadcasted_iota(jnp.int32, (16, cut), 1)
                drop = None
                for j in range(self.seg_count):
                    d = p - starts[0, j]
                    hit = (d >= 0) & (d < DILATION_SIZE)
                    drop = hit if drop is None else drop | hit
                keep = jnp.where(drop, 0.0, 1.0).astype(BF16)
                km[c * cut : (c + 1) * cut, :] = dot_tn(keep, spread.astype(BF16)).astype(BF16)

        def make_extra():
            cut = 1024
            n = self.misc_rows
            for c in range(steps // cut):
                at = pl.ds(c * cut, cut)
                p = t * steps + c * cut + lax.broadcasted_iota(jnp.int32, (1, cut), 1)
                speaker = jnp.full((1, cut), ids[0, 0], jnp.int32)
                for j in range(1, self.seg_count):
                    speaker = jnp.where(p >= starts[0, j], ids[0, j], speaker)
                wide_speaker = jnp.broadcast_to(speaker, (n, cut))
                for q in range(4):
                    row = lax.broadcasted_iota(jnp.int32, (n, self.cond_dim), 0)
                    col = lax.broadcasted_iota(jnp.int32, (n, self.cond_dim), 1)
                    pick = (col == row + q * self.cond_rows) & (row < self.cond_rows)
                    pick = jnp.where(pick, 1.0, 0.0).astype(BF16)
                    mel = dot_nn(pick, cn[:, at])
                    slot = lax.broadcasted_iota(jnp.int32, (n, cut), 0) - self.table_at
                    ours = (slot >= 0) & (slot < self.table_rows)
                    hot = ours & (slot + q * self.table_rows == wide_speaker)
                    part = jnp.where(hot, 1.0, mel)
                    et[q * n : (q + 1) * n, at] = part.astype(BF16)

        def flip_extra():
            cut = 1024
            for c in range(steps // cut):
                at = pl.ds(c * cut, cut)
                extra[at, :] = et[:, at].T

        def shift(at, value):
            keep = jnp.concatenate([km[at, :]] * (ch // LANES), axis=1)
            taps[0, at, :] = value * keep

        def prev_head():
            shift(pl.ds(0, DILATION_SIZE), b["halo"][...])

        def prev_rest():
            size = (steps - DILATION_SIZE) // 4

            def body(i):
                at = rows_at(i * size, size)
                shift(rows_at(i * size + DILATION_SIZE, size), taps[1, at, :])

            loop(4, body)

        body_rows = steps - DILATION_SIZE

        def mixture_first(block, between=lambda: None):
            size = body_rows // 2
            cols = pl.ds(pl.multiple_of(256 * block, 256), 256)

            def body(i):
                at = rows_at(i * size + DILATION_SIZE, size)
                w = wall[pl.ds(2 * zhigh, 2), 0:256, cols].reshape(ch, 256)
                act[at, cols] = dot_nn(taps[zhigh, at, :], w)
                pl.when(i == 0)(between)

            loop(2, body)

        def mixture(block, other=None, between=lambda: None):
            size = body_rows // 2
            cols = pl.ds(pl.multiple_of(256 * block, 256), 256)
            is_gate = block // 2
            scale = jnp.where(is_gate == 1, 0.5, 1.0).astype(F32)
            c0 = pl.ds(pl.multiple_of(256 * lax.rem(block, 2), 256), 256)

            def body(i):
                at = rows_at(i * size + DILATION_SIZE, size)
                w = wall[pl.ds(2 - 2 * zhigh, 2), 0:256, cols].reshape(ch, 256)
                m = wall[:, 256 : self.BLOCK_ROWS, cols].reshape(4 * self.misc_rows, 256)
                x = act[at, cols] + dot_nn(taps[1 - zhigh, at, :], w) + dot_nn(extra[at, :], m)
                x = scale * jnp.tanh(scale * x) + (1.0 - scale)
                act[at, cols] = x
                if other is not None:
                    y = act[at, pl.ds(pl.multiple_of(256 * other, 256), 256)]
                    gated[at, c0] = (x * y).astype(BF16)
                pl.when(i == 0)(between)

            loop(2, body)

        def mixture_head():
            at = pl.ds(0, DILATION_SIZE)

            def body(i):
                def columns(block):
                    cols = pl.ds(pl.multiple_of(256 * block, 256), 256)
                    w = wall[:, 0:256, cols].reshape(2 * ch, 256)
                    m = wall[:, 256 : self.BLOCK_ROWS, cols].reshape(4 * self.misc_rows, 256)
                    x = dot_nn(taps[0, at, :], w[:ch]) + dot_nn(taps[1, at, :], w[ch:])
                    return cols, x + dot_nn(extra[at, :], m)

                c0, x = columns(i)
                c1, y = columns(i + 2)
                th, sg = jnp.tanh(x), 0.5 * jnp.tanh(0.5 * y) + 0.5
                act[at, c0] = th
                act[at, c1] = sg
                gated[at, c0] = (th * sg).astype(BF16)

            loop(2, body)

        def mixture_grad(half):
            size = 512
            w = wo[...].reshape(ch, 2 * ch)
            for i in range(half * 3, half * 3 + 3):
                at = pl.ds(i * size, size)
                q = dot_nt(agrad[at, :], w[:, :ch]) + dot_nt(skip[at, :], w[:, ch:])
                th, sg = act[at, :ch], act[at, ch:]
                g = th * sg
                mg[at, :ch] = (q * (sg - g * th)).astype(BF16)
                mg[at, ch:] = (q * (g - g * sg)).astype(BF16)

        def wtaps(first):
            return wall[first : first + 2, 0:256, :].reshape(ch, 2 * ch)

        def head_back():
            at = pl.ds(0, DILATION_SIZE)
            keep = jnp.concatenate([km[at, :].astype(F32)] * (ch // LANES), axis=1)
            b["phs"][...] = (keep * dot_nt(mg[at, :], wtaps(0))).astype(BF16)

        def head_send():
            @pl.when(t > 0)
            def _():
                halo_back().start()

        def own_ref(row):
            return (own, row) if row < 512 else (act, row - 512)

        def store_grad(start, value):
            at = pl.ds(start, 256)
            keep, row = own_ref(start)
            even = core == 0
            for k in range(4):
                left = value[:, 2 * k * LANES : (2 * k + 1) * LANES]
                right = value[:, (2 * k + 1) * LANES : (2 * k + 2) * LANES]
                cols = slice(k * LANES, (k + 1) * LANES)
                keep[pl.ds(row, 256), cols] = jnp.where(even, left, right)
                b["ss"][at, cols] = jnp.where(even, right, left).astype(BF16)

        def conv_grad(part):
            side, h = part % 2, part // 2
            lo = slice(h * 128, h * 128 + 128)
            hi = slice(256 + h * 128, 256 + h * 128 + 128)
            lhs = jnp.concatenate([taps[side, :, lo], taps[side, :, hi]], axis=1)
            store_grad(512 + 256 * part, dot_tn(lhs, mg[...]))

        def misc_grad():
            store_grad(1536, dot_nn(et[...], mg[...]))

        def out_grad(part):
            lhs = gated[:, 256 * part : 256 * (part + 1)]
            value = jnp.concatenate([dot_tn(lhs, agrad[...]), dot_tn(lhs, skip[...])], axis=1)
            store_grad(256 * part, value)

        def projected(which, i):
            size = steps // 2
            cols = slice(which * ch, (which + 1) * ch)
            at = pl.ds(i * size, size)
            value = dot_nn(gated[at, :], wo[:, :, cols].reshape(ch, ch))
            if which == 0:
                value = value + taps[1, at, :].astype(F32)
            (res, skip)[which][at, :] = value.astype(BF16)

        def audio_block(at, later):
            keep = jnp.concatenate([km[later, :].astype(F32)] * (ch // LANES), axis=1)
            total = agrad[at, :].astype(F32) + dot_nt(mg[at, :], wtaps(2))
            agrad[at, :] = (total + keep * dot_nt(mg[later, :], wtaps(0))).astype(BF16)

        def audio_main(i):
            size = (steps - DILATION_SIZE) // 4
            audio_block(pl.ds(i * size, size), pl.ds(i * size + DILATION_SIZE, size))

        def audio_last():
            @pl.when(t < 7)
            def _():
                halo_back().wait_recv()

            @pl.when(t == 7)
            def _():
                b["phr"][...] = jnp.zeros((DILATION_SIZE, ch), BF16)

            at = pl.ds(steps - DILATION_SIZE, DILATION_SIZE)
            total = agrad[at, :].astype(F32) + dot_nt(mg[at, :], wtaps(2))
            agrad[at, :] = (total + b["phr"][...].astype(F32)).astype(BF16)

        def r_copy(j, source, target, where, arrival):
            return pltpu.make_async_remote_copy(
                src_ref=source,
                dst_ref=target,
                send_sem=b["sent"].at[4 + arrival // 2],
                recv_sem=b["r_recv"].at[j, arrival],
                device_id=where,
                device_id_type=MESH,
            )

        def r_start(*args):
            r_copy(*args).start()

        def r_arrived(j, ref, arrival):
            r_copy(j, ref, ref, (sib, z), arrival).wait_recv()

        def part_rows(j, start, size):
            return rows_at(self.PARTS[j][0] + start, size)

        def pair_sum(j, start, size, block):
            ref, row = own_ref(self.PARTS[j][0])
            other = b["sr"][part_rows(j, start, size), lanes(block)].astype(F32)
            return ref[rows_at(row + start, size), lanes(block)] + other

        def r_s(j):
            at = part_rows(j, 0, self.PARTS[j][1])
            r_start(j, b["ss"].at[at, :], b["sr"].at[at, :], (sib, z), 0)

        def r_1(j):
            row, size, _ = self.PARTS[j]
            half = size // 2
            r_arrived(j, b["sr"].at[pl.ds(row, size), :], 0)
            at = pl.ds(row // 2, half)
            for i, where in enumerate(((tx, z), (ty, z))):
                b["r1s"][i, at, :] = pair_sum(j, i * half, half, chip_d).astype(BF16)
                r_start(j, b["r1s"].at[i, at, :], b["r1r"].at[i, at, :], where, 1)

        def r_3(j):
            row, size, _ = self.PARTS[j]
            half = size // 2
            up, low = pl.ds(row, half), pl.ds(row + half, half)
            at, every = pl.ds(row // 2, half), pl.ds(row, size)
            b["r3s"][0, up, :] = pair_sum(j, 0, half, chip_x).astype(BF16)
            b["r3s"][1, low, :] = pair_sum(j, half, half, chip_y).astype(BF16)
            r_arrived(j, b["r1r"].at[:, at, :], 1)
            b["r3s"][0, low, :] = (
                pair_sum(j, half, half, chip_x) + b["r1r"][1, at, :].astype(F32)
            ).astype(BF16)
            r_start(j, b["r3s"].at[0, every, :], b["r3r"].at[0, every, :], (tx, z), 2)
            b["r3s"][1, up, :] = (
                pair_sum(j, 0, half, chip_y) + b["r1r"][0, at, :].astype(F32)
            ).astype(BF16)
            r_start(j, b["r3s"].at[1, every, :], b["r3r"].at[1, every, :], (ty, z), 2)

        def plane_sum(j, start, size):
            at = part_rows(j, start, size)
            return (
                pair_sum(j, start, size, chip)
                + b["r3r"][0, at, :].astype(F32)
                + b["r3r"][1, at, :].astype(F32)
            )

        def final(j):
            if j < 2:
                return fout
            return fconv.at[pl.ds(128 * ((j - 2) // 2), 128), :] if j < 6 else fmisc

        def z_at(j, which):
            half = self.PARTS[j][1] // 2
            return lax.rem(which, 2) * half, half

        def z_slot(j):
            return pl.ds(128 * (j // 2), self.PARTS[j][1] // 2)

        def z_copy(j, d):
            source = b["zs"].at[part_rows(j, *z_at(j, zslab[d])), :]
            return r_copy(j, source, b["zr"].at[d - 1, z_slot(j), :], (t, zslab[d]), 3)

        def r_z(j):
            row, size, pair = self.PARTS[j]
            every = pl.ds(row, size)
            r_arrived(j, b["r3r"].at[:, every, :], 2)
            b["zs"][every, :] = plane_sum(j, 0, size).astype(BF16)

            @pl.when(zhigh == pair)
            def _():
                z_copy(j, 1).start()
                final(j)[...] = plane_sum(j, *z_at(j, z))

            @pl.when(zhigh != pair)
            def _():
                z_copy(j, 2).start()
                z_copy(j, 3).start()

        def r_f(j):
            @pl.when(zhigh == self.PARTS[j][2])
            def _():
                r_arrived(j, b["zr"].at[:, z_slot(j), :], 3)
                total = final(j)[...]
                for i in range(3):
                    total = total + b["zr"][i, z_slot(j), :].astype(F32)
                final(j)[...] = total

        def n_copy(peer):
            mine = b["squares"].at[4 * t + z]
            return pltpu.make_async_remote_copy(
                src_ref=mine,
                dst_ref=mine,
                send_sem=b["sent"].at[6],
                recv_sem=b["n_recv"],
                device_id=peer,
                device_id_type=MESH,
            )

        def norm_start():
            total = jnp.zeros((8, LANES), F32)
            for ref in (fconv, fmisc, fout):
                value = ref[...]
                total = total + jnp.sum((value * value).reshape(-1, 8, LANES), axis=0)
            b["squares"][4 * t + z] = jnp.sum(total, axis=0, keepdims=True)
            for peer in reversed(peers):
                n_copy(peer).start()

        def norm_end():
            arrived(b["squares"].at[0:31], b["n_recv"])
            norm[...] = jnp.sum(b["squares"][...], axis=0)

        for copy in scalars:
            copy.wait()
        make_mask()
        barrier_wait()
        g_start(0, 0, "x", "y")
        g_start(0, 1, "z")
        g_start(0, 0, "c0")
        g_start(0, 2, "z")
        large[1].wait()
        make_extra()
        g_start(0, 3, "z")
        g_start(0, 4, "z")
        flip_extra()
        o_first()
        large[0].wait()
        prev_rest()
        g_xy(0)
        g_z(1)
        g_core(0, 0)
        mixture_first(chip, lambda: g_z(2))
        o_xy()
        g_d(0)
        g_z(3)
        g_xy(1)
        g_z(4)
        g_core(2, 0)
        mixture_first(chip_y)
        g_xy(2)
        o_z()
        g_core(1, 0)
        mixture_first(chip_x)
        g_xy(3)
        g_xy(4)

        @pl.when(t < 7)
        def _():
            halo_in().start()

        g_d(1)
        g_core(0, 1)
        mixture(chip)
        g_d(2)
        g_core(3, 0)
        mixture_first(chip_d)
        g_core(2, 1)
        mixture(chip_y, chip, lambda: g_d(3))
        g_d(4)
        g_core(1, 1)
        mixture(chip_x)
        g_core(3, 1)
        mixture(chip_d, chip_x)

        @pl.when(t == 0)
        def _():
            b["halo"][...] = jnp.zeros((DILATION_SIZE, ch), BF16)

        @pl.when(t > 0)
        def _():
            halo_in().wait_recv()

        prev_head()
        mixture_head()
        large[2].wait()
        large[3].wait()
        out_grad(0)
        r_s(0)
        o_d()
        out_grad(1)
        r_1(0)
        r_s(1)
        o_core()
        mixture_grad(0)
        r_1(1)
        mixture_grad(1)
        r_3(0)
        conv_grad(0)
        r_3(1)
        r_s(2)
        conv_grad(1)
        r_1(2)
        r_s(3)
        conv_grad(2)
        r_z(0)
        r_1(3)
        r_s(4)
        conv_grad(3)
        r_3(2)
        r_z(1)
        r_1(4)
        r_s(5)
        misc_grad()
        r_3(3)
        r_1(5)
        r_s(6)
        r_s(7)
        head_back()
        r_3(4)
        r_f(0)
        projected(0, 0)
        r_1(6)
        r_1(7)
        r_z(2)
        audio_main(0)
        r_3(5)
        r_z(3)
        r_f(1)
        projected(0, 1)
        r_3(6)
        r_3(7)
        head_send()
        r_z(4)
        audio_main(1)
        r_z(5)
        r_f(2)
        projected(1, 0)
        r_f(3)
        r_z(6)
        r_z(7)
        audio_main(2)
        r_f(4)
        audio_main(3)
        r_f(5)
        r_f(6)
        r_f(7)
        norm_start()
        projected(1, 1)
        audio_last()
        norm_end()

        def left(i, ref):
            pltpu.make_async_remote_copy(
                src_ref=ref,
                dst_ref=ref,
                send_sem=b["sent"].at[i],
                recv_sem=b["n_recv"],
                device_id=(sib, z),
                device_id_type=MESH,
            ).wait_send()

        row = 2 * ch
        wall_bytes = 31 * 2 * self.BLOCK_ROWS * LANES
        wo_bytes = 31 * 2 * 128 * LANES
        block_bytes = 2 * self.GRAD_ROWS * LANES
        early = 5 * block_bytes
        late = 2 * block_bytes + 3 * block_bytes // 4
        for i, count in ((0, wall_bytes), (1, wo_bytes), (4, early), (5, late)):
            left(i, taps.at[0, pl.ds(0, count // row), :])
        left(6, b["squares"].at[0:31])

        @pl.when(t < 7)
        def _():
            halo_in().wait_send()

        @pl.when(t > 0)
        def _():
            halo_back().wait_send()

    def __call__(self, ids, starts, audio, conditioning, grad_res, grad_skip, conv_w, cond_w, table_w, out_w):
        steps, ch = self.steps, self.channels
        wide = pltpu.VMEM((steps, ch), BF16)
        anywhere = pl.BlockSpec(memory_space=pl.ANY)
        vmem = pl.BlockSpec(memory_space=pltpu.VMEM)
        return pl.pallas_call(
            self.kernel,
            out_shape=[
                wide,
                wide,
                wide,
                pltpu.VMEM((256, LANES), F32),
                pltpu.VMEM((self.misc_rows, LANES), F32),
                pltpu.VMEM((128, LANES), F32),
                pltpu.VMEM((1, LANES), F32),
            ],
            in_specs=[anywhere] * 10,
            out_specs=[vmem] * 7,
            scratch_shapes=list(self.scratch().values()),
            compiler_params=pltpu.CompilerParams(
                collective_id=0, has_side_effects=True, vmem_limit_bytes=54 * 2**20
            ),
            name="layer",
        )(ids, starts, audio, conditioning, grad_res, grad_skip, conv_w, cond_w, table_w, out_w)


def closing_kernel(cond_rows, table_at, table_rows, *refs):
    (res, skip, agrad, fconv, fmisc, fout, norm), refs = refs[:7], refs[7:]
    state, refs = refs[:12], refs[12:]
    (res_o, skip_o, agrad_o, prenorm_o), refs = refs[:4], refs[4:]
    new_o, new, (sems,) = refs[:12], refs[12:24], refs[24:]
    copies = []

    def write(source, target):
        copies.append(pltpu.make_async_copy(source, target, sems.at[len(copies)]))
        copies[-1].start()

    for source, target in ((res, res_o), (skip, skip_o), (agrad, agrad_o)):
        write(source, target.at[0])
    prenorm = jnp.sqrt(jnp.sum(norm[...], keepdims=True))
    prenorm_o[...] = prenorm
    factor = jnp.minimum(1.0, clip_level / (prenorm + 1e-06))
    grads = (
        fconv[...],
        fmisc[0:cond_rows, :],
        fmisc[table_at : table_at + table_rows, :],
        fout[...],
    )
    for k, grad in enumerate(grads):
        master, first, second = (state[3 * k + i][...] for i in range(3))
        for i, value in enumerate(adamw(grad, factor, master, first, second)):
            new[3 * k + i][...] = value
            write(new[3 * k + i], new_o[3 * k + i])
    for copy in copies:
        copy.wait()


def closing(layer, results, state):
    wide = jax.ShapeDtypeStruct((1, layer.steps, layer.channels), BF16)
    vmem = pl.BlockSpec(memory_space=pltpu.VMEM)
    anywhere = pl.BlockSpec(memory_space=pl.ANY)
    return pl.pallas_call(
        functools.partial(closing_kernel, layer.cond_rows, layer.table_at, layer.table_rows),
        out_shape=[wide, wide, wide, jax.ShapeDtypeStruct((1, 1), F32)]
        + [jax.ShapeDtypeStruct(a.shape, F32) for a in state],
        in_specs=[vmem] * 19,
        out_specs=[anywhere] * 3 + [vmem] + [anywhere] * 12,
        scratch_shapes=[pltpu.VMEM(a.shape, F32) for a in state] + [pltpu.SemaphoreType.DMA((15,))],
        compiler_params=pltpu.CompilerParams(vmem_limit_bytes=32 * 2**20),
        name="closing",
    )(*results, *state)


def on_device_kernels(
    audio,
    conditioning,
    speaker_ids,
    seg_starts,
    grad_residual,
    grad_skip,
    conv_weight,
    conv_first,
    conv_second,
    cond_weight,
    cond_first,
    cond_second,
    speaker_table,
    table_first,
    table_second,
    out_weight,
    out_first,
    out_second,
):
    layer = Layer(
        audio.shape[1],
        audio.shape[2],
        conditioning.shape[1],
        cond_weight.shape[0],
        speaker_table.shape[0],
        seg_starts.shape[1],
    )
    results = layer(
        speaker_ids,
        seg_starts,
        audio,
        conditioning,
        grad_residual,
        grad_skip,
        conv_weight,
        cond_weight,
        speaker_table,
        out_weight,
    )
    state = (
        conv_weight,
        conv_first,
        conv_second,
        cond_weight,
        cond_first,
        cond_second,
        speaker_table,
        table_first,
        table_second,
        out_weight,
        out_first,
        out_second,
    )
    done = closing(layer, results, state)
    return (done[0], done[1], done[2], done[3].reshape(()), *done[4:])


def passed_along(value, axis, steps):
    count = lax.axis_size(axis)
    first, last = (max(0, -steps), min(count, count - steps))
    return lax.ppermute(value, axis, [(source, source + steps) for source in range(first, last)])


def contract_rows(left, right):
    return lax.dot_general(
        left, right, (((0,), (0,)), ((), ())), preferred_element_type=jnp.float32
    )


def contract_cols(left, right):
    return lax.dot_general(
        left, right, (((1,), (1,)), ((), ())), preferred_element_type=jnp.float32
    )


def own_block(whole, shard):
    row_start = lax.axis_index("batch") * shard.shape[0]
    col_start = lax.axis_index("tm") * shard.shape[1]
    return lax.dynamic_slice(whole, (row_start, col_start), shard.shape)


def square_sum(matrix):
    return jnp.sum(matrix * matrix)


def on_device(
    audio,
    conditioning,
    speaker_ids,
    seg_starts,
    grad_residual,
    grad_skip,
    conv_weight,
    conv_first,
    conv_second,
    cond_weight,
    cond_first,
    cond_second,
    speaker_table,
    table_first,
    table_second,
    out_weight,
    out_first,
    out_second,
):
    rows_dev, steps_per_device, channels = audio.shape
    tokens = rows_dev * steps_per_device
    conv_rows, cond_rows, table_rows, out_rows = (
        lax.all_gather(conv_weight.astype(jnp.bfloat16), "batch", axis=0, tiled=True),
        lax.all_gather(cond_weight.astype(jnp.bfloat16), "batch", axis=0, tiled=True),
        lax.all_gather(speaker_table.astype(jnp.bfloat16), "batch", axis=0, tiled=True),
        lax.all_gather(out_weight.astype(jnp.bfloat16), "batch", axis=0, tiled=True),
    )
    conv_full, cond_full, table_full, out_full = (
        lax.all_gather(conv_rows, "tm", axis=1, tiled=True),
        lax.all_gather(cond_rows, "tm", axis=1, tiled=True),
        lax.all_gather(table_rows, "tm", axis=1, tiled=True),
        lax.all_gather(out_rows, "tm", axis=1, tiled=True),
    )
    offset = lax.axis_index("tm") * steps_per_device
    positions = offset + jnp.arange(steps_per_device, dtype=jnp.int32)
    seg_count = seg_starts.shape[1]
    segment = (
        jnp.sum((positions[None, :, None] >= seg_starts[:, None, :]).astype(jnp.int32), axis=2) - 1
    )
    seg_match = segment[:, :, None] == jnp.arange(seg_count, dtype=jnp.int32)[None, None, :]
    local_start = jnp.sum(jnp.where(seg_match, seg_starts[:, None, :], 0), axis=2)
    retain_mask = (positions[None, :] - DILATION_SIZE >= local_start).astype(jnp.bfloat16)
    seg_hot = seg_match.astype(jnp.bfloat16)
    speakers = table_full.shape[0]
    speaker_hot = (
        speaker_ids[:, :, None] == jnp.arange(speakers, dtype=jnp.int32)[None, None, :]
    ).astype(jnp.bfloat16)
    seg_embed = jnp.einsum(
        "rsk,kf->rsf", speaker_hot, table_full, preferred_element_type=jnp.float32
    ).astype(jnp.bfloat16)
    tail_input = passed_along(audio[:, steps_per_device - DILATION_SIZE :, :], "tm", 1)
    previous = (
        jnp.concatenate([tail_input, audio[:, : steps_per_device - DILATION_SIZE, :]], axis=1)
        * retain_mask[:, :, None]
    )
    flat_audio = audio.reshape(tokens, channels)
    flat_prev = previous.reshape(tokens, channels)
    mixture = jnp.dot(flat_prev, conv_full[:channels], preferred_element_type=jnp.float32)
    mixture = mixture + jnp.dot(
        flat_audio, conv_full[channels:], preferred_element_type=jnp.float32
    )
    mixture = mixture + jnp.einsum(
        "rct,cf->rtf", conditioning, cond_full, preferred_element_type=jnp.float32
    ).reshape(tokens, -1)
    mixture = mixture + jnp.einsum(
        "rts,rsf->rtf", seg_hot, seg_embed, preferred_element_type=jnp.float32
    ).reshape(tokens, -1)
    filter_tanh = jnp.tanh(mixture[:, :channels])
    gate_sig = jax.nn.sigmoid(mixture[:, channels:])
    gated_out = (filter_tanh * gate_sig).astype(jnp.bfloat16)
    projected = jnp.dot(gated_out, out_full, preferred_element_type=jnp.float32)
    residual_out = (
        (flat_audio.astype(jnp.float32) + projected[:, :channels])
        .astype(jnp.bfloat16)
        .reshape(audio.shape)
    )
    skip_out = projected[:, channels:].astype(jnp.bfloat16).reshape(audio.shape)
    back_out = jnp.concatenate(
        [grad_residual.reshape(tokens, channels), grad_skip.reshape(tokens, channels)], axis=1
    )
    out_grad = contract_rows(gated_out, back_out)
    gated_grad = contract_cols(back_out, out_full)
    filter_grad = gated_grad * gate_sig * (1.0 - filter_tanh * filter_tanh)
    gate_grad = gated_grad * filter_tanh * gate_sig * (1.0 - gate_sig)
    mixture_grad = jnp.concatenate([filter_grad, gate_grad], axis=1).astype(jnp.bfloat16)
    conv_grad = jnp.concatenate(
        [contract_rows(flat_prev, mixture_grad), contract_rows(flat_audio, mixture_grad)], axis=0
    )
    grad_blocks = mixture_grad.reshape(rows_dev, steps_per_device, -1)
    cond_grad = jnp.einsum(
        "rct,rtf->cf", conditioning, grad_blocks, preferred_element_type=jnp.float32
    )
    seg_sums = jnp.einsum("rts,rtf->rsf", seg_hot, grad_blocks, preferred_element_type=jnp.float32)
    table_grad = jnp.einsum(
        "rsk,rsf->kf",
        speaker_hot.astype(jnp.float32),
        seg_sums,
        precision=lax.Precision.HIGHEST,
        preferred_element_type=jnp.float32,
    )
    preceding_gradient = (
        contract_cols(mixture_grad, conv_full[:channels]).reshape(audio.shape)
        * retain_mask[:, :, None]
    ).astype(jnp.bfloat16)
    head_input = passed_along(preceding_gradient[:, :DILATION_SIZE, :], "tm", -1)
    later_contribution = jnp.concatenate(
        [preceding_gradient[:, DILATION_SIZE:, :], head_input], axis=1
    ).astype(jnp.float32)
    current_tap = contract_cols(mixture_grad, conv_full[channels:]).reshape(audio.shape)
    audio_grad = (grad_residual.astype(jnp.float32) + current_tap + later_contribution).astype(
        jnp.bfloat16
    )
    conv_total, cond_total, table_total, out_total = lax.psum(
        (conv_grad, cond_grad, table_grad, out_grad), ("tm", "batch")
    )
    squares = (
        square_sum(conv_total)
        + square_sum(cond_total)
        + square_sum(table_total)
        + square_sum(out_total)
    )
    conv_part = own_block(conv_total, conv_weight)
    cond_part = own_block(cond_total, cond_weight)
    table_part = own_block(table_total, speaker_table)
    out_part = own_block(out_total, out_weight)
    prenorm = jnp.sqrt(squares)
    factor = jnp.minimum(1.0, clip_level / (prenorm + 1e-06))
    conv_state = adamw(conv_part, factor, conv_weight, conv_first, conv_second)
    cond_state = adamw(cond_part, factor, cond_weight, cond_first, cond_second)
    table_state = adamw(table_part, factor, speaker_table, table_first, table_second)
    out_state = adamw(out_part, factor, out_weight, out_first, out_second)
    return (
        residual_out,
        skip_out,
        audio_grad,
        prenorm,
        conv_state[0],
        conv_state[1],
        conv_state[2],
        cond_state[0],
        cond_state[1],
        cond_state[2],
        table_state[0],
        table_state[1],
        table_state[2],
        out_state[0],
        out_state[1],
        out_state[2],
    )


def solution(mesh):
    placed = (
        P("batch", "tm", None),
        P("batch", None, "tm"),
        P("batch", None),
        P("batch", None),
        P("batch", "tm", None),
        P("batch", "tm", None),
        P("batch", "tm"),
        P("batch", "tm"),
        P("batch", "tm"),
        P("batch", "tm"),
        P("batch", "tm"),
        P("batch", "tm"),
        P("batch", "tm"),
        P("batch", "tm"),
        P("batch", "tm"),
        P("batch", "tm"),
        P("batch", "tm"),
        P("batch", "tm"),
    )
    small = mesh.shape["tm"] == 8 and mesh.shape["batch"] == 4
    return jax.shard_map(
        on_device_kernels if small else on_device,
        mesh=mesh,
        in_specs=placed,
        out_specs=(
            P("batch", "tm", None),
            P("batch", "tm", None),
            P("batch", "tm", None),
            P(),
            P("batch", "tm"),
            P("batch", "tm"),
            P("batch", "tm"),
            P("batch", "tm"),
            P("batch", "tm"),
            P("batch", "tm"),
            P("batch", "tm"),
            P("batch", "tm"),
            P("batch", "tm"),
            P("batch", "tm"),
            P("batch", "tm"),
            P("batch", "tm"),
        ),
        check_vma=False,
    )
```
